32 devices in a mesh: grp: 2 (over y), ctg: 4 (over z), line: 4 (over x, core).
Axes of the slice: x: 2, y: 2, z: 4, core: 2. Of those that a mesh axis runs over, the one named last changes fastest.
Arguments:
- owned_flow: float32 [4, 24, 5120], P('line', 'grp', 'ctg'), parts along dimension 1, may hold values from -6 to 6
- ratings: float32 [20480], P('line'), may hold values from 0.8 to 3
- lodf_tiles: bfloat16 [4, 32, 128, 128], P('ctg', 'line'), may hold values from -2.5 to 2.5
- tile_map: int32 [4, 160], P('ctg', 'line'), may hold values from -1 to 7, as said below
- outage_line: int32 [512], P('ctg'), may hold values from 0 to 20479, as said below
- block_owner: int32 [4], replicated, may hold values from 0 to 3, each once
- multipliers: float32 [4, 32, 24, 128, 128], P('ctg', 'line', 'grp'), parts along dimension 2, may hold values from 0.05 to 2
Outputs:
- new_multipliers: float32 [4, 32, 24, 128, 128], P('ctg', 'line', 'grp'), parts along dimension 2
- line_gradient: float32 [4, 24, 5120], P('line', 'grp', 'ctg'), parts along dimension 1
- outage_gradient: float32 [24, 512], P('grp', 'ctg'), parts along dimension 0
The draws below stay inside these ranges and needn't reach their ends.
There are 2 independent parts, one for each index of `grp`. The reference program is written for one: setup_inputs(seed, part) draws one part's arguments, and reference() takes and returns one part's arrays. A program takes and returns all parts, laid end to end along the dimension named above; an argument that names none is the same for every part. Nothing has to cross between parts.
Inputs may be any that keep to these rules, and one draw needn't show every extreme that they name: `tile_map`: in each row and each run of B = 40 columns of a line shard, the slots 0 to n - 1 appear once each for some n of at least 2, and the other entries are -1; every line shard has n = 8 in some row. `outage_line`: no two contingencies take out the same line. `block_owner`: each owner slot names a different block.
All inputs are finite; a program needn't handle non-finite values.
Results may differ from the reference program's by a relative error of at most 0.0003.
Values sent between devices are 32-bit elements; how exact they have to be, the bound alone decides.
A program may use at most 128 MiB of HBM per device.

```python
import math
import jax
import jax.numpy as jnp
from jax import lax

LINES = 20480
TILE = 128
SLOTS = 8
HOURS = 12
OUTAGES = 512
N_CTG = 4
N_LINE = 4


def draw_tile_map(key, part):
    key = jax.random.fold_in(key, 11)
    count_key, full_key, order_key = jax.random.split(key, 3)
    kblocks = OUTAGES // TILE
    blocks = LINES // (TILE * N_LINE)
    lower = max(1, SLOTS // 3)
    counts = jax.random.randint(count_key, (kblocks, N_LINE), lower, SLOTS + 1)
    full_row = jax.random.randint(full_key, (N_LINE,), 0, kblocks)
    rows = jnp.arange(kblocks, dtype=jnp.int32)[:, None]
    counts = jnp.where(rows == full_row[None, :], SLOTS, counts)
    order_keys = jax.random.split(order_key, kblocks * N_LINE)
    orders = jax.vmap(lambda single: jax.random.permutation(single, blocks))(order_keys)
    ranks = jnp.argsort(orders, axis=1).astype(jnp.int32).reshape(kblocks, N_LINE, blocks)
    chosen = jnp.where(ranks < counts[:, :, None], ranks, -1)
    return chosen.reshape(kblocks, N_LINE * blocks).astype(jnp.int32)


def draw_outage_line(key, part):
    key = jax.random.fold_in(key, 12)
    return jax.random.permutation(key, LINES)[:OUTAGES].astype(jnp.int32)


def shard_levels(key, shape, shards, low, largest):
    def one(axis_at, shards_of):
        steps = jax.random.uniform(jax.random.fold_in(jax.random.fold_in(key, 6), axis_at), (shards_of,), jnp.float32, low / len(shards), largest / len(shards))
        return jnp.repeat(jnp.exp(steps), shape[axis_at] // shards_of).reshape((-1,) + (1,) * (len(shape) - axis_at - 1))

    level = one(*shards[0])
    for cut in shards[1:]:
        level = level * one(*cut)
    return level


def normal_values(key, extent, spread, most, cuts=(), kind=jnp.bfloat16):
    loudness = shard_levels(key, extent, cuts, -0.22, 0.18) if cuts else 1.0
    drawn = jax.random.normal(key, extent, jnp.float32) * spread * loudness
    return jnp.minimum(jnp.maximum(drawn, -most), most).astype(kind)


def setup_inputs(seed: int = 0, part: int = 0) -> dict:
    key_list = jax.random.split(jax.random.key(seed), 8)
    part_splits = jax.random.split(jax.random.fold_in(key_list[7], part), 8)
    return {
        "owned_flow": normal_values(part_splits[0], (N_LINE, HOURS, LINES // N_LINE), 1.0, 6.0, ((0, 4), (2, 4)), jnp.float32),
        "ratings": jnp.clip(jnp.exp(math.log(3.0) - 1.3217558 * jax.random.uniform(key_list[1], (LINES,), jnp.float32) ** shard_levels(key_list[1], (LINES,), ((0, 4),), -0.2, 0.2)), 0.8, 3.0),
        "lodf_tiles": normal_values(key_list[2], (OUTAGES // TILE, N_LINE * SLOTS, TILE, TILE), 0.4, 2.5, ((0, 4), (1, 4))),
        "tile_map": draw_tile_map(jax.random.fold_in(key_list[7], 71), part),
        "outage_line": draw_outage_line(jax.random.fold_in(key_list[7], 71), part),
        "block_owner": jax.random.permutation(key_list[5], N_CTG).astype(jnp.int32),
        "multipliers": jnp.clip(jnp.exp(math.log(2.0) - 3.6888794 * jax.random.uniform(part_splits[6], (OUTAGES // TILE, N_LINE * SLOTS, HOURS, TILE, TILE), jnp.float32) ** shard_levels(part_splits[6], (OUTAGES // TILE, N_LINE * SLOTS, HOURS, TILE, TILE), ((0, 4), (1, 4)), -0.2, 0.2)), 0.05, 2.0),
    }


dual_step = 0.5
outage_scale = 0.0625


def tile_step(tiles, slot_map, flow_rows, rating_rows, outage_flow, multipliers):
    slots = tiles.shape[0]
    match = (slot_map[:, None] == jnp.arange(slots, dtype=jnp.int32)[None, :]).astype(jnp.float32)
    slot_flow = jnp.einsum("bs,hbl->shl", match, flow_rows, precision=lax.Precision.HIGHEST)
    slot_rating = jnp.einsum("bs,bl->sl", match, rating_rows, precision=lax.Precision.HIGHEST)
    present = jnp.sum(match, axis=0)
    safe_rating = slot_rating + (1.0 - present)[:, None]
    inverse = 1.0 / (safe_rating * safe_rating)
    lodf = tiles.astype(jnp.float32)
    post = slot_flow[:, :, None, :] + lodf[:, None, :, :] * outage_flow[None, :, :, None]
    raised = multipliers + dual_step * (post * post * inverse[:, None, None, :] - 1.0)
    updated = jnp.maximum(raised, 0.0) * present[:, None, None, None]
    weight = updated * post * inverse[:, None, None, :]
    direct = jnp.sum(weight, axis=2)
    line_part = jnp.einsum("bs,shl->hbl", match, direct, precision=lax.Precision.HIGHEST)
    outage_part = jnp.sum(lodf[:, None, :, :] * weight, axis=(0, 3))
    return updated, line_part, outage_part


def reference(owned_flow, ratings, lodf_tiles, tile_map, outage_line, block_owner, multipliers):
    hours = owned_flow.shape[1]
    shard_lines = LINES // N_LINE
    piece = shard_lines // N_CTG
    blocks = shard_lines // TILE
    kblocks = OUTAGES // TILE
    inverse_owner = jnp.zeros_like(block_owner).at[block_owner].set(jnp.arange(N_CTG, dtype=jnp.int32))
    shaped = jnp.take(owned_flow.reshape(N_LINE, hours, N_CTG, piece), inverse_owner, axis=2)
    flow = shaped.transpose(1, 0, 2, 3).reshape(hours, LINES)
    outage_flow = jnp.take(flow, outage_line, axis=1)
    flow_rows = flow.reshape(hours, N_LINE, blocks, TILE)
    rating_rows = ratings.reshape(N_LINE, blocks, TILE)
    tiles = lodf_tiles.reshape(kblocks, N_LINE, SLOTS, TILE, TILE)
    maps = tile_map.reshape(kblocks, N_LINE, blocks)
    mults = multipliers.reshape(kblocks, N_LINE, SLOTS, hours, TILE, TILE)
    outage_blocks = outage_flow.reshape(hours, kblocks, TILE).transpose(1, 0, 2)

    def one_block(items):
        tile_group, map_group, outage_group, mult_group = items
        return jax.vmap(tile_step, in_axes=(0, 0, 1, 0, None, 0))(
            tile_group, map_group, flow_rows, rating_rows, outage_group, mult_group)

    updated, line_part, outage_part = lax.map(one_block, (tiles, maps, outage_blocks, mults))
    line_gradient = jnp.sum(line_part, axis=0).reshape(N_LINE, hours, shard_lines) / OUTAGES
    outage_gradient = jnp.sum(outage_part, axis=1).transpose(1, 0, 2).reshape(hours, OUTAGES) * outage_scale
    new_multipliers = updated.reshape(kblocks, N_LINE * SLOTS, hours, TILE, TILE)
    return new_multipliers, line_gradient, outage_gradient
```

```python
import functools

import jax
import jax.numpy as jnp
from jax import lax
from jax.experimental import pallas as pl
from jax.experimental.pallas import tpu as pltpu
from jax.sharding import PartitionSpec as P

dual_step = 0.5
outage_scale = 0.0625
MESH = pl.DeviceIdType.MESH
LANES = 128
ROWS = 8


def tile_step(tiles, slot_map, flow_rows, rating_rows, outage_flow, multipliers):
    slots = tiles.shape[0]
    match = (slot_map[:, None] == jnp.arange(slots, dtype=jnp.int32)[None, :]).astype(jnp.float32)
    slot_flow = jnp.einsum("bs,hbl->shl", match, flow_rows, precision=lax.Precision.HIGHEST)
    slot_rating = jnp.einsum("bs,bl->sl", match, rating_rows, precision=lax.Precision.HIGHEST)
    present = jnp.sum(match, axis=0)
    safe_rating = slot_rating + (1.0 - present)[:, None]
    inverse = 1.0 / (safe_rating * safe_rating)
    lodf = tiles.astype(jnp.float32)
    post = slot_flow[:, :, None, :] + lodf[:, None, :, :] * outage_flow[None, :, :, None]
    raised = multipliers + dual_step * (post * post * inverse[:, None, None, :] - 1.0)
    updated = jnp.maximum(raised, 0.0) * present[:, None, None, None]
    weight = updated * post * inverse[:, None, None, :]
    direct = jnp.sum(weight, axis=2)
    line_part = jnp.einsum("bs,shl->hbl", match, direct, precision=lax.Precision.HIGHEST)
    outage_part = jnp.sum(lodf[:, None, :, :] * weight, axis=(0, 3))
    return (updated, line_part, outage_part)


def per_device_general(owned_flow, ratings, lodf_tiles, tile_map, outage_line, block_owner, multipliers):
    hours = owned_flow.shape[1]
    piece = owned_flow.shape[2]
    ctg_count = lax.axis_size("ctg")
    line_count = lax.axis_size("line")
    shard_lines = ratings.shape[0]
    tile = lodf_tiles.shape[-1]
    kblocks = lodf_tiles.shape[0]
    outages = outage_line.shape[0] * ctg_count
    inverse_owner = (
        jnp.zeros_like(block_owner).at[block_owner].set(jnp.arange(ctg_count, dtype=jnp.int32))
    )
    gathered = lax.all_gather(owned_flow, ("ctg", "line"), axis=0, tiled=True)
    shaped = jnp.take(gathered.reshape(ctg_count, line_count, hours, piece), inverse_owner, axis=0)
    every_flow = shaped.transpose(2, 1, 0, 3).reshape(hours, line_count * shard_lines)
    shard_flow = lax.dynamic_slice_in_dim(
        every_flow, lax.axis_index("line") * shard_lines, shard_lines, 1
    )
    outage_flow = jnp.take(every_flow, outage_line, axis=1)
    flow_rows = shard_flow.reshape(hours, shard_lines // tile, tile)
    rating_rows = ratings.reshape(shard_lines // tile, tile)
    outage_blocks = outage_flow.reshape(hours, kblocks, tile).transpose(1, 0, 2)
    updated, line_part, outage_part = jax.vmap(tile_step, in_axes=(0, 0, None, None, 0, 0))(
        lodf_tiles, tile_map, flow_rows, rating_rows, outage_blocks, multipliers
    )
    line_sum = jnp.sum(line_part, axis=0).reshape(hours, shard_lines)
    line_gradient = (
        lax.psum_scatter(
            line_sum.reshape(1, hours, shard_lines), "ctg", scatter_dimension=2, tiled=True
        )
        / outages
    )
    outage_local = outage_part.transpose(1, 0, 2).reshape(hours, kblocks * tile)
    outage_gradient = lax.psum(outage_local, "line") * outage_scale
    return (updated, line_gradient, outage_gradient)


def kernel(
    n_ctg, n_line, outages,
    map_hbm, owner_hbm, outage_hbm, rating_hbm, own_hbm, lodf_hbm, mult_hbm,
    new_ref, line_ref, grad_ref,
    map_ref, owner_ref, outage_ref, rating_ref,
    mult, lodf16, lodf, flows, onehot, slot_flow, slot_half, slot_bar, spread, acc, direct,
    map_send, map_recv, part, grad,
    small_sem, mult_sem, lodf_sem, own_sem, flow_ssem, flow_rsem, map_ssem, map_rsem,
    part_ssem, part_rsem, dir_ssem, dir_rsem, grad_ssem, grad_rsem,
):
    slots, hours, tile, _ = mult.shape
    inner = flows.shape[1] // hours
    piece = inner * tile
    me_c = lax.axis_index("ctg")
    me_l = lax.axis_index("line")

    def other_c(d):
        return lax.rem(me_c + d, n_ctg)

    def other_l(d):
        return lax.rem(me_l + d, n_line)

    barrier = pltpu.get_barrier_semaphore()
    for d in range(1, n_ctg):
        pl.semaphore_signal(barrier, inc=1, device_id={"ctg": other_c(d)}, device_id_type=MESH)
    for d in range(1, n_line):
        pl.semaphore_signal(barrier, inc=1, device_id={"line": other_l(d)}, device_id_type=MESH)

    own_copy = pltpu.make_async_copy(own_hbm, flows.at[me_c], own_sem)
    own_copy.start()
    small_copies = [
        pltpu.make_async_copy(src, dst, small_sem.at[i])
        for i, (src, dst) in enumerate(
            ((map_hbm, map_ref), (owner_hbm, owner_ref), (outage_hbm, outage_ref), (rating_hbm, rating_ref))
        )
    ]
    for copy in small_copies:
        copy.start()
    lodf_copy = pltpu.make_async_copy(lodf_hbm.at[0], lodf16, lodf_sem)
    lodf_copy.start()
    for s in range(slots):
        pltpu.make_async_copy(mult_hbm.at[0, s], mult.at[s], mult_sem.at[s]).start()

    for copy in small_copies:
        copy.wait()
    for q in range(n_ctg):
        for i in range(inner):
            map_send[q, pl.ds(i, 1), :] = jnp.full((1, LANES), map_ref[0, q * inner + i], jnp.int32)
    own_copy.wait()
    pl.semaphore_wait(barrier, n_ctg - 1 + n_line - 1)

    flow_copies = []
    for d in range(1, n_ctg):
        copy = pltpu.make_async_remote_copy(
            src_ref=flows.at[me_c], dst_ref=flows.at[me_c],
            send_sem=flow_ssem.at[d], recv_sem=flow_rsem.at[d],
            device_id={"ctg": other_c(d)}, device_id_type=MESH,
        )
        copy.start()
        flow_copies.append(copy)
    map_copies = []
    for d in range(1, n_ctg):
        copy = pltpu.make_async_remote_copy(
            src_ref=map_send.at[other_c(d)], dst_ref=map_recv.at[me_c],
            send_sem=map_ssem.at[d], recv_sem=map_rsem.at[d],
            device_id={"ctg": other_c(d)}, device_id_type=MESH,
        )
        copy.start()
        map_copies.append(copy)
    map_recv[me_c] = map_send[me_c]

    rows_iota = lax.broadcasted_iota(jnp.int32, (tile, LANES), 0)
    for c in range(n_ctg):
        base = (me_l * n_ctg + owner_ref[c]) * piece
        wanted = jnp.broadcast_to(outage_ref[...] - base, (tile, LANES))

        def hot_body(b, carry, c=c, wanted=wanted):
            row = pl.multiple_of(b * tile, tile)
            hit = (rows_iota + row) == wanted
            onehot[c, pl.ds(row, tile), :] = jnp.where(hit, 1.0, 0.0).astype(jnp.bfloat16)
            return carry

        lax.fori_loop(0, inner, hot_body, 0)

    slot_iota = lax.broadcasted_iota(jnp.int32, (slots, LANES), 0)
    rating = jnp.ones((slots, LANES), jnp.float32)
    there = jnp.zeros((slots, LANES), jnp.float32)
    for b in range(n_ctg * inner):
        hit = slot_iota == map_ref[0, b]
        rating = jnp.where(hit, jnp.broadcast_to(rating_ref[pl.ds(b, 1), :], (slots, LANES)), rating)
        there = jnp.where(hit, 1.0, there)
    slot_half[...] = there * (dual_step / (rating * rating))
    slot_bar[...] = jnp.where(there > 0.0, dual_step, 1e30)

    lodf_copy.wait()

    def lodf_body(s, carry):
        lodf[s] = lodf16[s].astype(jnp.float32)
        return carry

    lax.fori_loop(0, slots, lodf_body, 0)
    acc[...] = jnp.zeros_like(acc)

    def pick(c):
        value = jnp.concatenate(
            [flows[c, pl.ds(i, hours, stride=inner), :] for i in range(inner)], axis=1
        )
        high = value.astype(jnp.bfloat16)
        rest = value - high.astype(jnp.float32)
        middle = rest.astype(jnp.bfloat16)
        low = (rest - middle.astype(jnp.float32)).astype(jnp.bfloat16)
        table = onehot[c]
        total = jnp.dot(high, table, preferred_element_type=jnp.float32)
        total = total + jnp.dot(middle, table, preferred_element_type=jnp.float32)
        return total + jnp.dot(low, table, preferred_element_type=jnp.float32)

    def place(c, found):
        hits = []
        for i in range(inner):
            block = jnp.int32(-1)
            for q in range(n_ctg):
                block = jnp.where(owner_ref[c] == q, map_ref[0, q * inner + i], block)
            hits.append(slot_iota == block)
        out = []
        for t in range(hours):
            rows = found[t]
            for i in range(inner):
                row = flows[c, pl.ds(t * inner + i, 1), :]
                rows = jnp.where(hits[i], jnp.broadcast_to(row, (slots, LANES)), rows)
            out.append(rows)
        return out

    order = [me_c]
    picked = pick(me_c)
    for d in (1, 3, 2) if n_ctg == 4 else range(1, n_ctg):
        flow_copies[d - 1].wait_recv()
        order.append(lax.rem(me_c + n_ctg - d, n_ctg))
        picked = picked + pick(order[-1])
    part[me_l] = picked
    part_copies = []
    for d in range(1, n_line):
        copy = pltpu.make_async_remote_copy(
            src_ref=part.at[me_l], dst_ref=part.at[me_l],
            send_sem=part_ssem.at[d], recv_sem=part_rsem.at[d],
            device_id={"line": other_l(d)}, device_id_type=MESH,
        )
        copy.start()
        part_copies.append(copy)

    found = [jnp.zeros((slots, LANES), jnp.float32)] * hours
    for c in range(n_ctg):
        found = place(c, found)
    for t in range(hours):
        slot_flow[t] = found[t]

    for copy in part_copies:
        copy.wait_recv()
    outage = part[0]
    for j in range(1, n_line):
        outage = outage + part[j]
    turned = jnp.concatenate([outage, jnp.zeros((16 - hours, LANES), jnp.float32)], axis=0).T
    for t in range(hours):
        spread[t] = jnp.broadcast_to(turned[:, t : t + 1], (tile, LANES))

    def direct_copy(s, d):
        return pltpu.make_async_remote_copy(
            src_ref=direct.at[me_c, s], dst_ref=direct.at[me_c, s],
            send_sem=dir_ssem.at[s, d], recv_sem=dir_rsem.at[s, d],
            device_id={"ctg": other_c(d)}, device_id_type=MESH,
        )

    def slot_body(s, carry):
        pltpu.make_async_copy(mult_hbm.at[0, s], mult.at[s], mult_sem.at[s]).wait()
        half = jnp.broadcast_to(slot_half[pl.ds(s, 1), :], (ROWS, LANES))
        bar = jnp.broadcast_to(slot_bar[pl.ds(s, 1), :], (ROWS, LANES))
        base = [
            jnp.broadcast_to(slot_flow[t, pl.ds(s, 1), :], (ROWS, LANES)) for t in range(hours)
        ]

        def row_body(k, sums):
            row = pl.multiple_of(k * ROWS, ROWS)
            factor = lodf[s, pl.ds(row, ROWS), :]
            out = []
            for t in range(hours):
                post = base[t] + factor * spread[t, pl.ds(row, ROWS), :]
                scaled = post * half
                updated = jnp.maximum(mult[s, t, pl.ds(row, ROWS), :] + (post * scaled - bar), 0.0)
                new_ref[s, t, pl.ds(row, ROWS), :] = updated
                weight = updated * scaled
                acc[t, pl.ds(row, ROWS), :] += factor * weight
                out.append(sums[t] + weight)
            return tuple(out)

        zero = jnp.zeros((ROWS, LANES), jnp.float32)
        sums = lax.fori_loop(0, tile // ROWS, row_body, (zero,) * hours)
        for t in range(hours):
            direct[me_c, s, pl.ds(t, 1), :] = jnp.sum(sums[t], axis=0, keepdims=True)
        for d in range(1, n_ctg):
            direct_copy(s, d).start()
        return carry

    lax.fori_loop(0, slots, slot_body, 0)

    columns = lax.broadcasted_iota(jnp.int32, (tile, LANES), 1)
    packed = jnp.zeros((tile, LANES), jnp.float32)
    for t in range(hours):
        packed = jnp.where(columns == t, jnp.sum(acc[t], axis=1, keepdims=True), packed)
    grad[me_l] = packed.T[:hours]
    grad_copies = []
    for d in range(1, n_line):
        copy = pltpu.make_async_remote_copy(
            src_ref=grad.at[me_l], dst_ref=grad.at[me_l],
            send_sem=grad_ssem.at[d], recv_sem=grad_rsem.at[d],
            device_id={"line": other_l(d)}, device_id_type=MESH,
        )
        copy.start()
        grad_copies.append(copy)

    for copy in map_copies:
        copy.wait_recv()

    def direct_wait(s, carry):
        for d in range(1, n_ctg):
            direct_copy(s, d).wait()
        return carry

    lax.fori_loop(0, slots, direct_wait, 0)

    for i in range(inner):
        total = jnp.zeros((hours, LANES), jnp.float32)
        for c in range(n_ctg):
            which = jnp.broadcast_to(map_recv[c, pl.ds(i, 1), :], (hours, LANES))
            found = jnp.zeros((hours, LANES), jnp.float32)
            for s in range(slots):
                found = jnp.where(which == s, direct[c, s], found)
            total = total + found
        line_ref[pl.ds(i, hours, stride=inner), :] = total * (1.0 / dual_step / outages)

    for copy in grad_copies:
        copy.wait_recv()
    total = grad[0]
    for j in range(1, n_line):
        total = total + grad[j]
    grad_ref[...] = total * (outage_scale / dual_step)

    for copy in flow_copies + map_copies + part_copies + grad_copies:
        copy.wait_send()


def per_device_fused(owned_flow, ratings, lodf_tiles, tile_map, outage_line, block_owner, multipliers):
    n_ctg = lax.axis_size("ctg")
    n_line = lax.axis_size("line")
    _, hours, piece = owned_flow.shape
    _, slots, tile, _ = lodf_tiles.shape
    inner = piece // tile
    outages = outage_line.shape[0] * n_ctg
    f32, bf16, i32 = jnp.float32, jnp.bfloat16, jnp.int32
    dma = pltpu.SemaphoreType.DMA
    vmem = pl.BlockSpec(memory_space=pltpu.VMEM)
    hbm = pl.BlockSpec(memory_space=pltpu.HBM)
    updated, line_gradient, outage_gradient = pl.pallas_call(
        functools.partial(kernel, n_ctg, n_line, outages),
        out_shape=(
            jax.ShapeDtypeStruct((slots, hours, tile, tile), f32),
            jax.ShapeDtypeStruct((hours * inner, tile), f32),
            jax.ShapeDtypeStruct((hours, tile), f32),
        ),
        in_specs=[hbm] * 7,
        out_specs=(vmem, vmem, vmem),
        scratch_shapes=[
            pltpu.SMEM(tile_map.shape, i32),
            pltpu.SMEM(block_owner.shape, i32),
            pltpu.VMEM((1, tile), i32),
            pltpu.VMEM((n_ctg * inner, tile), f32),
            pltpu.VMEM((slots, hours, tile, tile), f32),
            pltpu.VMEM((slots, tile, tile), bf16),
            pltpu.VMEM((slots, tile, tile), f32),
            pltpu.VMEM((n_ctg, hours * inner, tile), f32),
            pltpu.VMEM((n_ctg, piece, tile), bf16),
            pltpu.VMEM((hours, slots, tile), f32),
            pltpu.VMEM((slots, tile), f32),
            pltpu.VMEM((slots, tile), f32),
            pltpu.VMEM((hours, tile, tile), f32),
            pltpu.VMEM((hours, tile, tile), f32),
            pltpu.VMEM((n_ctg, slots, hours, tile), f32),
            pltpu.VMEM((n_ctg, inner, tile), i32),
            pltpu.VMEM((n_ctg, inner, tile), i32),
            pltpu.VMEM((n_line, hours, tile), f32),
            pltpu.VMEM((n_line, hours, tile), f32),
            dma((4,)), dma((slots,)), dma, dma,
            dma((n_ctg,)), dma((n_ctg,)), dma((n_ctg,)), dma((n_ctg,)),
            dma((n_line,)), dma((n_line,)),
            dma((slots, n_ctg)), dma((slots, n_ctg)),
            dma((n_line,)), dma((n_line,)),
        ],
        compiler_params=pltpu.CompilerParams(
            collective_id=0, has_side_effects=True, vmem_limit_bytes=40 * 1024 * 1024
        ),
        name="dual_step",
    )(
        tile_map, block_owner, outage_line.reshape(1, tile), ratings.reshape(n_ctg * inner, tile),
        owned_flow.reshape(hours * inner, tile), lodf_tiles, multipliers,
    )
    return updated[None], line_gradient.reshape(1, hours, piece), outage_gradient


def per_device(owned_flow, ratings, lodf_tiles, tile_map, outage_line, block_owner, multipliers):
    n_ctg = lax.axis_size("ctg")
    tile = lodf_tiles.shape[-1]
    whole = (
        tile == LANES
        and owned_flow.shape[1] <= 16
        and owned_flow.shape[2] % tile == 0
        and outage_line.shape[0] == tile
        and lodf_tiles.shape[0] == 1
        and n_ctg <= 4
    )
    form = per_device_fused if whole else per_device_general
    return form(owned_flow, ratings, lodf_tiles, tile_map, outage_line, block_owner, multipliers)


def solution(mesh):
    placed = (
        P("line", "grp", "ctg"),
        P("line"),
        P("ctg", "line", None, None),
        P("ctg", "line"),
        P("ctg"),
        P(),
        P("ctg", "line", "grp", None, None),
    )
    return jax.shard_map(
        per_device,
        mesh=mesh,
        in_specs=placed,
        out_specs=(P("ctg", "line", "grp", None, None), P("line", "grp", "ctg"), P("grp", "ctg")),
        check_vma=False,
    )
```

```python
import functools

import jax
import jax.numpy as jnp
from jax import lax
from jax.experimental import pallas as pl
from jax.experimental.pallas import tpu as pltpu
from jax.sharding import PartitionSpec as P

dual_step = 0.5
outage_scale = 0.0625
MESH = pl.DeviceIdType.MESH
LANES = 128
ROWS = 8


def tile_step(tiles, slot_map, flow_rows, rating_rows, outage_flow, multipliers):
    slots = tiles.shape[0]
    match = (slot_map[:, None] == jnp.arange(slots, dtype=jnp.int32)[None, :]).astype(jnp.float32)
    slot_flow = jnp.einsum("bs,hbl->shl", match, flow_rows, precision=lax.Precision.HIGHEST)
    slot_rating = jnp.einsum("bs,bl->sl", match, rating_rows, precision=lax.Precision.HIGHEST)
    present = jnp.sum(match, axis=0)
    safe_rating = slot_rating + (1.0 - present)[:, None]
    inverse = 1.0 / (safe_rating * safe_rating)
    lodf = tiles.astype(jnp.float32)
    post = slot_flow[:, :, None, :] + lodf[:, None, :, :] * outage_flow[None, :, :, None]
    raised = multipliers + dual_step * (post * post * inverse[:, None, None, :] - 1.0)
    updated = jnp.maximum(raised, 0.0) * present[:, None, None, None]
    weight = updated * post * inverse[:, None, None, :]
    direct = jnp.sum(weight, axis=2)
    line_part = jnp.einsum("bs,shl->hbl", match, direct, precision=lax.Precision.HIGHEST)
    outage_part = jnp.sum(lodf[:, None, :, :] * weight, axis=(0, 3))
    return (updated, line_part, outage_part)


def per_device_general(owned_flow, ratings, lodf_tiles, tile_map, outage_line, block_owner, multipliers):
    hours = owned_flow.shape[1]
    piece = owned_flow.shape[2]
    ctg_count = lax.axis_size("ctg")
    line_count = lax.axis_size("line")
    shard_lines = ratings.shape[0]
    tile = lodf_tiles.shape[-1]
    kblocks = lodf_tiles.shape[0]
    outages = outage_line.shape[0] * ctg_count
    inverse_owner = (
        jnp.zeros_like(block_owner).at[block_owner].set(jnp.arange(ctg_count, dtype=jnp.int32))
    )
    gathered = lax.all_gather(owned_flow, ("ctg", "line"), axis=0, tiled=True)
    shaped = jnp.take(gathered.reshape(ctg_count, line_count, hours, piece), inverse_owner, axis=0)
    every_flow = shaped.transpose(2, 1, 0, 3).reshape(hours, line_count * shard_lines)
    shard_flow = lax.dynamic_slice_in_dim(
        every_flow, lax.axis_index("line") * shard_lines, shard_lines, 1
    )
    outage_flow = jnp.take(every_flow, outage_line, axis=1)
    flow_rows = shard_flow.reshape(hours, shard_lines // tile, tile)
    rating_rows = ratings.reshape(shard_lines // tile, tile)
    outage_blocks = outage_flow.reshape(hours, kblocks, tile).transpose(1, 0, 2)
    updated, line_part, outage_part = jax.vmap(tile_step, in_axes=(0, 0, None, None, 0, 0))(
        lodf_tiles, tile_map, flow_rows, rating_rows, outage_blocks, multipliers
    )
    line_sum = jnp.sum(line_part, axis=0).reshape(hours, shard_lines)
    line_gradient = (
        lax.psum_scatter(
            line_sum.reshape(1, hours, shard_lines), "ctg", scatter_dimension=2, tiled=True
        )
        / outages
    )
    outage_local = outage_part.transpose(1, 0, 2).reshape(hours, kblocks * tile)
    outage_gradient = lax.psum(outage_local, "line") * outage_scale
    return (updated, line_gradient, outage_gradient)


def kernel(
    n_ctg, n_line, outages,
    map_hbm, owner_hbm, outage_hbm, rating_hbm, own_hbm, lodf_hbm, mult_hbm,
    new_ref, line_ref, grad_ref,
    map_ref, owner_ref, outage_ref, rating_ref,
    mult, lodf16, lodf, flows, onehot, slot_flow, slot_half, slot_bar, spread, acc, direct,
    map_send, map_recv, part, grad,
    small_sem, mult_sem, lodf_sem, own_sem, flow_ssem, flow_rsem, map_ssem, map_rsem,
    part_ssem, part_rsem, dir_ssem, dir_rsem, grad_ssem, grad_rsem,
):
    slots, hours, tile, _ = mult.shape
    inner = flows.shape[1] // hours
    piece = inner * tile
    me_c = lax.axis_index("ctg")
    me_l = lax.axis_index("line")

    def other_c(d):
        return lax.rem(me_c + d, n_ctg)

    def other_l(d):
        return lax.rem(me_l + d, n_line)

    barrier = pltpu.get_barrier_semaphore()
    for d in range(1, n_ctg):
        pl.semaphore_signal(barrier, inc=1, device_id={"ctg": other_c(d)}, device_id_type=MESH)
    for d in range(1, n_line):
        pl.semaphore_signal(barrier, inc=1, device_id={"line": other_l(d)}, device_id_type=MESH)

    own_copy = pltpu.make_async_copy(own_hbm, flows.at[me_c], own_sem)
    own_copy.start()
    small_copies = [
        pltpu.make_async_copy(src, dst, small_sem.at[i])
        for i, (src, dst) in enumerate(
            ((map_hbm, map_ref), (owner_hbm, owner_ref), (outage_hbm, outage_ref), (rating_hbm, rating_ref))
        )
    ]
    for copy in small_copies:
        copy.start()
    lodf_copy = pltpu.make_async_copy(lodf_hbm.at[0], lodf16, lodf_sem)
    lodf_copy.start()
    for s in range(slots):
        pltpu.make_async_copy(mult_hbm.at[0, s], mult.at[s], mult_sem.at[s]).start()

    for copy in small_copies:
        copy.wait()
    for q in range(n_ctg):
        for i in range(inner):
            map_send[q, pl.ds(i, 1), :] = jnp.full((1, LANES), map_ref[0, q * inner + i], jnp.int32)
    own_copy.wait()
    pl.semaphore_wait(barrier, n_ctg - 1 + n_line - 1)

    flow_copies = []
    for d in range(1, n_ctg):
        copy = pltpu.make_async_remote_copy(
            src_ref=flows.at[me_c], dst_ref=flows.at[me_c],
            send_sem=flow_ssem.at[d], recv_sem=flow_rsem.at[d],
            device_id={"ctg": other_c(d)}, device_id_type=MESH,
        )
        copy.start()
        flow_copies.append(copy)
    map_copies = []
    for d in range(1, n_ctg):
        copy = pltpu.make_async_remote_copy(
            src_ref=map_send.at[other_c(d)], dst_ref=map_recv.at[me_c],
            send_sem=map_ssem.at[d], recv_sem=map_rsem.at[d],
            device_id={"ctg": other_c(d)}, device_id_type=MESH,
        )
        copy.start()
        map_copies.append(copy)
    map_recv[me_c] = map_send[me_c]

    rows_iota = lax.broadcasted_iota(jnp.int32, (tile, LANES), 0)
    for c in range(n_ctg):
        base = (me_l * n_ctg + owner_ref[c]) * piece
        wanted = jnp.broadcast_to(outage_ref[...] - base, (tile, LANES))

        def hot_body(b, carry, c=c, wanted=wanted):
            row = pl.multiple_of(b * tile, tile)
            hit = (rows_iota + row) == wanted
            onehot[c, pl.ds(row, tile), :] = jnp.where(hit, 1.0, 0.0).astype(jnp.bfloat16)
            return carry

        lax.fori_loop(0, inner, hot_body, 0)

    slot_iota = lax.broadcasted_iota(jnp.int32, (slots, LANES), 0)
    rating = jnp.ones((slots, LANES), jnp.float32)
    there = jnp.zeros((slots, LANES), jnp.float32)
    for b in range(n_ctg * inner):
        hit = slot_iota == map_ref[0, b]
        rating = jnp.where(hit, jnp.broadcast_to(rating_ref[pl.ds(b, 1), :], (slots, LANES)), rating)
        there = jnp.where(hit, 1.0, there)
    slot_half[...] = there * (dual_step / (rating * rating))
    slot_bar[...] = jnp.where(there > 0.0, dual_step, 1e30)

    lodf_copy.wait()

    def lodf_body(s, carry):
        lodf[s] = lodf16[s].astype(jnp.float32)
        return carry

    lax.fori_loop(0, slots, lodf_body, 0)
    acc[...] = jnp.zeros_like(acc)

    def pick(c):
        value = jnp.concatenate(
            [flows[c, pl.ds(i, hours, stride=inner), :] for i in range(inner)], axis=1
        )
        high = value.astype(jnp.bfloat16)
        rest = value - high.astype(jnp.float32)
        middle = rest.astype(jnp.bfloat16)
        low = (rest - middle.astype(jnp.float32)).astype(jnp.bfloat16)
        table = onehot[c]
        total = jnp.dot(high, table, preferred_element_type=jnp.float32)
        total = total + jnp.dot(middle, table, preferred_element_type=jnp.float32)
        return total + jnp.dot(low, table, preferred_element_type=jnp.float32)

    def place(c, found):
        hits = []
        for i in range(inner):
            block = jnp.int32(-1)
            for q in range(n_ctg):
                block = jnp.where(owner_ref[c] == q, map_ref[0, q * inner + i], block)
            hits.append(slot_iota == block)
        out = []
        for t in range(hours):
            rows = found[t]
            for i in range(inner):
                row = flows[c, pl.ds(t * inner + i, 1), :]
                rows = jnp.where(hits[i], jnp.broadcast_to(row, (slots, LANES)), rows)
            out.append(rows)
        return out

    order = [me_c]
    picked = pick(me_c)
    for d in (1, 3, 2) if n_ctg == 4 else range(1, n_ctg):
        flow_copies[d - 1].wait_recv()
        order.append(lax.rem(me_c + n_ctg - d, n_ctg))
        picked = picked + pick(order[-1])
    part[me_l] = picked
    part_copies = []
    for d in range(1, n_line):
        copy = pltpu.make_async_remote_copy(
            src_ref=part.at[me_l], dst_ref=part.at[me_l],
            send_sem=part_ssem.at[d], recv_sem=part_rsem.at[d],
            device_id={"line": other_l(d)}, device_id_type=MESH,
        )
        copy.start()
        part_copies.append(copy)

    found = [jnp.zeros((slots, LANES), jnp.float32)] * hours
    for c in range(n_ctg):
        found = place(c, found)
    for t in range(hours):
        slot_flow[t] = found[t]

    for copy in part_copies:
        copy.wait_recv()
    outage = part[0]
    for j in range(1, n_line):
        outage = outage + part[j]
    turned = jnp.concatenate([outage, jnp.zeros((16 - hours, LANES), jnp.float32)], axis=0).T
    for t in range(hours):
        spread[t] = jnp.broadcast_to(turned[:, t : t + 1], (tile, LANES))

    def direct_copy(s, d):
        return pltpu.make_async_remote_copy(
            src_ref=direct.at[me_c, s], dst_ref=direct.at[me_c, s],
            send_sem=dir_ssem.at[s, d], recv_sem=dir_rsem.at[s, d],
            device_id={"ctg": other_c(d)}, device_id_type=MESH,
        )

    def slot_body(s, carry):
        pltpu.make_async_copy(mult_hbm.at[0, s], mult.at[s], mult_sem.at[s]).wait()
        half = jnp.broadcast_to(slot_half[pl.ds(s, 1), :], (ROWS, LANES))
        bar = jnp.broadcast_to(slot_bar[pl.ds(s, 1), :], (ROWS, LANES))
        base = [
            jnp.broadcast_to(slot_flow[t, pl.ds(s, 1), :], (ROWS, LANES)) for t in range(hours)
        ]

        def row_body(k, sums):
            row = pl.multiple_of(k * ROWS, ROWS)
            factor = lodf[s, pl.ds(row, ROWS), :]
            out = []
            for t in range(hours):
                post = base[t] + factor * spread[t, pl.ds(row, ROWS), :]
                scaled = post * half
                updated = jnp.maximum(mult[s, t, pl.ds(row, ROWS), :] + (post * scaled - bar), 0.0)
                new_ref[s, t, pl.ds(row, ROWS), :] = updated
                weight = updated * scaled
                acc[t, pl.ds(row, ROWS), :] += factor * weight
                out.append(sums[t] + weight)
            return tuple(out)

        zero = jnp.zeros((ROWS, LANES), jnp.float32)
        sums = lax.fori_loop(0, tile // ROWS, row_body, (zero,) * hours)
        for t in range(hours):
            direct[me_c, s, pl.ds(t, 1), :] = jnp.sum(sums[t], axis=0, keepdims=True)
        for d in range(1, n_ctg):
            direct_copy(s, d).start()
        return carry

    lax.fori_loop(0, slots, slot_body, 0)

    columns = lax.broadcasted_iota(jnp.int32, (tile, LANES), 1)
    packed = jnp.zeros((tile, LANES), jnp.float32)
    for t in range(hours):
        packed = jnp.where(columns == t, jnp.sum(acc[t], axis=1, keepdims=True), packed)
    grad[me_l] = packed.T[:hours]
    grad_copies = []
    for d in range(1, n_line):
        copy = pltpu.make_async_remote_copy(
            src_ref=grad.at[me_l], dst_ref=grad.at[me_l],
            send_sem=grad_ssem.at[d], recv_sem=grad_rsem.at[d],
            device_id={"line": other_l(d)}, device_id_type=MESH,
        )
        copy.start()
        grad_copies.append(copy)

    for copy in map_copies:
        copy.wait_recv()

    def direct_wait(s, carry):
        for d in range(1, n_ctg):
            direct_copy(s, d).wait()
        return carry

    lax.fori_loop(0, slots, direct_wait, 0)

    for i in range(inner):
        total = jnp.zeros((hours, LANES), jnp.float32)
        for c in range(n_ctg):
            which = jnp.broadcast_to(map_recv[c, pl.ds(i, 1), :], (hours, LANES))
            found = jnp.zeros((hours, LANES), jnp.float32)
            for s in range(slots):
                found = jnp.where(which == s, direct[c, s], found)
            total = total + found
        line_ref[pl.ds(i, hours, stride=inner), :] = total * (1.0 / dual_step / outages)

    for copy in grad_copies:
        copy.wait_recv()
    total = grad[0]
    for j in range(1, n_line):
        total = total + grad[j]
    grad_ref[...] = total * (outage_scale / dual_step)

    for copy in flow_copies + map_copies + part_copies + grad_copies:
        copy.wait_send()


def per_device_fused(owned_flow, ratings, lodf_tiles, tile_map, outage_line, block_owner, multipliers):
    n_ctg = lax.axis_size("ctg")
    n_line = lax.axis_size("line")
    _, hours, piece = owned_flow.shape
    _, slots, tile, _ = lodf_tiles.shape
    inner = piece // tile
    outages = outage_line.shape[0] * n_ctg
    f32, bf16, i32 = jnp.float32, jnp.bfloat16, jnp.int32
    dma = pltpu.SemaphoreType.DMA
    vmem = pl.BlockSpec(memory_space=pltpu.VMEM)
    hbm = pl.BlockSpec(memory_space=pltpu.HBM)
    updated, line_gradient, outage_gradient = pl.pallas_call(
        functools.partial(kernel, n_ctg, n_line, outages),
        out_shape=(
            jax.ShapeDtypeStruct((slots, hours, tile, tile), f32),
            jax.ShapeDtypeStruct((hours * inner, tile), f32),
            jax.ShapeDtypeStruct((hours, tile), f32),
        ),
        in_specs=[hbm] * 7,
        out_specs=(vmem, vmem, vmem),
        scratch_shapes=[
            pltpu.SMEM(tile_map.shape, i32),
            pltpu.SMEM(block_owner.shape, i32),
            pltpu.VMEM((1, tile), i32),
            pltpu.VMEM((n_ctg * inner, tile), f32),
            pltpu.VMEM((slots, hours, tile, tile), f32),
            pltpu.VMEM((slots, tile, tile), bf16),
            pltpu.VMEM((slots, tile, tile), f32),
            pltpu.VMEM((n_ctg, hours * inner, tile), f32),
            pltpu.VMEM((n_ctg, piece, tile), bf16),
            pltpu.VMEM((hours, slots, tile), f32),
            pltpu.VMEM((slots, tile), f32),
            pltpu.VMEM((slots, tile), f32),
            pltpu.VMEM((hours, tile, tile), f32),
            pltpu.VMEM((hours, tile, tile), f32),
            pltpu.VMEM((n_ctg, slots, hours, tile), f32),
            pltpu.VMEM((n_ctg, inner, tile), i32),
            pltpu.VMEM((n_ctg, inner, tile), i32),
            pltpu.VMEM((n_line, hours, tile), f32),
            pltpu.VMEM((n_line, hours, tile), f32),
            dma((4,)), dma((slots,)), dma, dma,
            dma((n_ctg,)), dma((n_ctg,)), dma((n_ctg,)), dma((n_ctg,)),
            dma((n_line,)), dma((n_line,)),
            dma((slots, n_ctg)), dma((slots, n_ctg)),
            dma((n_line,)), dma((n_line,)),
        ],
        compiler_params=pltpu.CompilerParams(
            collective_id=0, has_side_effects=True, vmem_limit_bytes=62 * 1024 * 1024
        ),
        name="dual_step",
    )(
        tile_map, block_owner, outage_line.reshape(1, tile), ratings.reshape(n_ctg * inner, tile),
        owned_flow.reshape(hours * inner, tile), lodf_tiles, multipliers,
    )
    return updated[None], line_gradient.reshape(1, hours, piece), outage_gradient


def per_device(owned_flow, ratings, lodf_tiles, tile_map, outage_line, block_owner, multipliers):
    n_ctg = lax.axis_size("ctg")
    tile = lodf_tiles.shape[-1]
    whole = (
        tile == LANES
        and owned_flow.shape[1] <= 16
        and owned_flow.shape[2] % tile == 0
        and outage_line.shape[0] == tile
        and lodf_tiles.shape[0] == 1
        and n_ctg <= 4
    )
    form = per_device_fused if whole else per_device_general
    return form(owned_flow, ratings, lodf_tiles, tile_map, outage_line, block_owner, multipliers)


def solution(mesh):
    placed = (
        P("line", "grp", "ctg"),
        P("line"),
        P("ctg", "line", None, None),
        P("ctg", "line"),
        P("ctg"),
        P(),
        P("ctg", "line", "grp", None, None),
    )
    return jax.shard_map(
        per_device,
        mesh=mesh,
        in_specs=placed,
        out_specs=(P("ctg", "line", "grp", None, None), P("line", "grp", "ctg"), P("grp", "ctg")),
        check_vma=False,
    )
```

```python
import functools

import jax
import jax.numpy as jnp
from jax import lax
from jax.experimental import pallas as pl
from jax.experimental.pallas import tpu as pltpu
from jax.sharding import PartitionSpec as P

dual_step = 0.5
outage_scale = 0.0625
MESH = pl.DeviceIdType.MESH
LANES = 128
ROWS = 8


def tile_step(tiles, slot_map, flow_rows, rating_rows, outage_flow, multipliers):
    slots = tiles.shape[0]
    match = (slot_map[:, None] == jnp.arange(slots, dtype=jnp.int32)[None, :]).astype(jnp.float32)
    slot_flow = jnp.einsum("bs,hbl->shl", match, flow_rows, precision=lax.Precision.HIGHEST)
    slot_rating = jnp.einsum("bs,bl->sl", match, rating_rows, precision=lax.Precision.HIGHEST)
    present = jnp.sum(match, axis=0)
    safe_rating = slot_rating + (1.0 - present)[:, None]
    inverse = 1.0 / (safe_rating * safe_rating)
    lodf = tiles.astype(jnp.float32)
    post = slot_flow[:, :, None, :] + lodf[:, None, :, :] * outage_flow[None, :, :, None]
    raised = multipliers + dual_step * (post * post * inverse[:, None, None, :] - 1.0)
    updated = jnp.maximum(raised, 0.0) * present[:, None, None, None]
    weight = updated * post * inverse[:, None, None, :]
    direct = jnp.sum(weight, axis=2)
    line_part = jnp.einsum("bs,shl->hbl", match, direct, precision=lax.Precision.HIGHEST)
    outage_part = jnp.sum(lodf[:, None, :, :] * weight, axis=(0, 3))
    return (updated, line_part, outage_part)


def per_device_general(owned_flow, ratings, lodf_tiles, tile_map, outage_line, block_owner, multipliers):
    hours = owned_flow.shape[1]
    piece = owned_flow.shape[2]
    ctg_count = lax.axis_size("ctg")
    line_count = lax.axis_size("line")
    shard_lines = ratings.shape[0]
    tile = lodf_tiles.shape[-1]
    kblocks = lodf_tiles.shape[0]
    outages = outage_line.shape[0] * ctg_count
    inverse_owner = (
        jnp.zeros_like(block_owner).at[block_owner].set(jnp.arange(ctg_count, dtype=jnp.int32))
    )
    gathered = lax.all_gather(owned_flow, ("ctg", "line"), axis=0, tiled=True)
    shaped = jnp.take(gathered.reshape(ctg_count, line_count, hours, piece), inverse_owner, axis=0)
    every_flow = shaped.transpose(2, 1, 0, 3).reshape(hours, line_count * shard_lines)
    shard_flow = lax.dynamic_slice_in_dim(
        every_flow, lax.axis_index("line") * shard_lines, shard_lines, 1
    )
    outage_flow = jnp.take(every_flow, outage_line, axis=1)
    flow_rows = shard_flow.reshape(hours, shard_lines // tile, tile)
    rating_rows = ratings.reshape(shard_lines // tile, tile)
    outage_blocks = outage_flow.reshape(hours, kblocks, tile).transpose(1, 0, 2)
    updated, line_part, outage_part = jax.vmap(tile_step, in_axes=(0, 0, None, None, 0, 0))(
        lodf_tiles, tile_map, flow_rows, rating_rows, outage_blocks, multipliers
    )
    line_sum = jnp.sum(line_part, axis=0).reshape(hours, shard_lines)
    line_gradient = (
        lax.psum_scatter(
            line_sum.reshape(1, hours, shard_lines), "ctg", scatter_dimension=2, tiled=True
        )
        / outages
    )
    outage_local = outage_part.transpose(1, 0, 2).reshape(hours, kblocks * tile)
    outage_gradient = lax.psum(outage_local, "line") * outage_scale
    return (updated, line_gradient, outage_gradient)


def kernel(
    n_ctg, n_line, outages,
    map_hbm, owner_hbm, outage_hbm, rating_hbm, own_hbm, lodf_hbm, mult_hbm,
    new_ref, line_ref, grad_ref,
    map_ref, owner_ref, outage_ref, rating_ref,
    mult, lodf16, lodf, flows, onehot, slot_flow, slot_half, slot_bar, spread, acc, direct,
    map_send, map_recv, part, grad,
    small_sem, mult_sem, lodf_sem, own_sem, flow_ssem, flow_rsem, map_ssem, map_rsem,
    part_ssem, part_rsem, dir_ssem, dir_rsem, grad_ssem, grad_rsem,
):
    slots, hours, tile, _ = mult.shape
    inner = flows.shape[1] // hours
    piece = inner * tile
    me_c = lax.axis_index("ctg")
    me_l = lax.axis_index("line")

    def other_c(d):
        return lax.rem(me_c + d, n_ctg)

    def other_l(d):
        return lax.rem(me_l + d, n_line)

    barrier = pltpu.get_barrier_semaphore()
    for d in range(1, n_ctg):
        pl.semaphore_signal(barrier, inc=1, device_id={"ctg": other_c(d)}, device_id_type=MESH)
    for d in range(1, n_line):
        pl.semaphore_signal(barrier, inc=1, device_id={"line": other_l(d)}, device_id_type=MESH)

    own_copy = pltpu.make_async_copy(own_hbm, flows.at[me_c], own_sem)
    own_copy.start()
    small_copies = [
        pltpu.make_async_copy(src, dst, small_sem.at[i])
        for i, (src, dst) in enumerate(
            ((map_hbm, map_ref), (owner_hbm, owner_ref), (outage_hbm, outage_ref), (rating_hbm, rating_ref))
        )
    ]
    for copy in small_copies:
        copy.start()
    lodf_copy = pltpu.make_async_copy(lodf_hbm.at[0], lodf16, lodf_sem)
    lodf_copy.start()
    for s in range(slots):
        pltpu.make_async_copy(mult_hbm.at[0, s], mult.at[s], mult_sem.at[s]).start()

    for copy in small_copies:
        copy.wait()
    for q in range(n_ctg):
        for i in range(inner):
            map_send[q, pl.ds(i, 1), :] = jnp.full((1, LANES), map_ref[0, q * inner + i], jnp.int32)
    own_copy.wait()
    pl.semaphore_wait(barrier, n_ctg - 1 + n_line - 1)

    flow_copies = []
    for d in range(1, n_ctg):
        copy = pltpu.make_async_remote_copy(
            src_ref=flows.at[me_c], dst_ref=flows.at[me_c],
            send_sem=flow_ssem.at[d], recv_sem=flow_rsem.at[d],
            device_id={"ctg": other_c(d)}, device_id_type=MESH,
        )
        copy.start()
        flow_copies.append(copy)
    map_copies = []
    for d in range(1, n_ctg):
        copy = pltpu.make_async_remote_copy(
            src_ref=map_send.at[other_c(d)], dst_ref=map_recv.at[me_c],
            send_sem=map_ssem.at[d], recv_sem=map_rsem.at[d],
            device_id={"ctg": other_c(d)}, device_id_type=MESH,
        )
        copy.start()
        map_copies.append(copy)
    map_recv[me_c] = map_send[me_c]

    rows_iota = lax.broadcasted_iota(jnp.int32, (tile, LANES), 0)
    for c in range(n_ctg):
        base = (me_l * n_ctg + owner_ref[c]) * piece
        wanted = jnp.broadcast_to(outage_ref[...] - base, (tile, LANES))

        def hot_body(b, carry, c=c, wanted=wanted):
            row = pl.multiple_of(b * tile, tile)
            hit = (rows_iota + row) == wanted
            onehot[c, pl.ds(row, tile), :] = jnp.where(hit, 1.0, 0.0).astype(jnp.bfloat16)
            return carry

        lax.fori_loop(0, inner, hot_body, 0)

    slot_iota = lax.broadcasted_iota(jnp.int32, (slots, LANES), 0)
    rating = jnp.ones((slots, LANES), jnp.float32)
    there = jnp.zeros((slots, LANES), jnp.float32)
    for b in range(n_ctg * inner):
        hit = slot_iota == map_ref[0, b]
        rating = jnp.where(hit, jnp.broadcast_to(rating_ref[pl.ds(b, 1), :], (slots, LANES)), rating)
        there = jnp.where(hit, 1.0, there)
    slot_half[...] = there * (dual_step / (rating * rating))
    slot_bar[...] = jnp.where(there > 0.0, dual_step, 1e30)

    lodf_copy.wait()

    def lodf_body(s, carry):
        lodf[s] = lodf16[s].astype(jnp.float32)
        return carry

    lax.fori_loop(0, slots, lodf_body, 0)
    acc[...] = jnp.zeros_like(acc)

    def pick(c):
        value = jnp.concatenate(
            [flows[c, pl.ds(i, hours, stride=inner), :] for i in range(inner)], axis=1
        )
        high = value.astype(jnp.bfloat16)
        rest = value - high.astype(jnp.float32)
        middle = rest.astype(jnp.bfloat16)
        low = (rest - middle.astype(jnp.float32)).astype(jnp.bfloat16)
        table = onehot[c]
        total = jnp.dot(high, table, preferred_element_type=jnp.float32)
        total = total + jnp.dot(middle, table, preferred_element_type=jnp.float32)
        return total + jnp.dot(low, table, preferred_element_type=jnp.float32)

    def place(c, found):
        hits = []
        for i in range(inner):
            block = jnp.int32(-1)
            for q in range(n_ctg):
                block = jnp.where(owner_ref[c] == q, map_ref[0, q * inner + i], block)
            hits.append(slot_iota == block)
        out = []
        for t in range(hours):
            rows = found[t]
            for i in range(inner):
                row = flows[c, pl.ds(t * inner + i, 1), :]
                rows = jnp.where(hits[i], jnp.broadcast_to(row, (slots, LANES)), rows)
            out.append(rows)
        return out

    order = [me_c]
    picked = pick(me_c)
    for d in (1, 3, 2) if n_ctg == 4 else range(1, n_ctg):
        flow_copies[d - 1].wait_recv()
        order.append(lax.rem(me_c + n_ctg - d, n_ctg))
        picked = picked + pick(order[-1])
    part[me_l] = picked
    part_copies = []
    for d in range(1, n_line):
        copy = pltpu.make_async_remote_copy(
            src_ref=part.at[me_l], dst_ref=part.at[me_l],
            send_sem=part_ssem.at[d], recv_sem=part_rsem.at[d],
            device_id={"line": other_l(d)}, device_id_type=MESH,
        )
        copy.start()
        part_copies.append(copy)

    found = [jnp.zeros((slots, LANES), jnp.float32)] * hours
    for c in range(n_ctg):
        found = place(c, found)
    for t in range(hours):
        slot_flow[t] = found[t]

    for copy in part_copies:
        copy.wait_recv()
    outage = part[0]
    for j in range(1, n_line):
        outage = outage + part[j]
    turned = jnp.concatenate([outage, jnp.zeros((16 - hours, LANES), jnp.float32)], axis=0).T
    for t in range(hours):
        spread[t] = jnp.broadcast_to(turned[:, t : t + 1], (tile, LANES))

    def direct_copy(s, d):
        return pltpu.make_async_remote_copy(
            src_ref=direct.at[me_c, s], dst_ref=direct.at[me_c, s],
            send_sem=dir_ssem.at[s, d], recv_sem=dir_rsem.at[s, d],
            device_id={"ctg": other_c(d)}, device_id_type=MESH,
        )

    def slot_body(s, carry):
        pltpu.make_async_copy(mult_hbm.at[0, s], mult.at[s], mult_sem.at[s]).wait()
        half = jnp.broadcast_to(slot_half[pl.ds(s, 1), :], (ROWS, LANES))
        bar = jnp.broadcast_to(slot_bar[pl.ds(s, 1), :], (ROWS, LANES))
        base = [
            jnp.broadcast_to(slot_flow[t, pl.ds(s, 1), :], (ROWS, LANES)) for t in range(hours)
        ]

        def row_body(k, sums):
            row = pl.multiple_of(k * ROWS, ROWS)
            factor = lodf[s, pl.ds(row, ROWS), :]
            out = []
            for t in range(hours):
                post = base[t] + factor * spread[t, pl.ds(row, ROWS), :]
                scaled = post * half
                updated = jnp.maximum(mult[s, t, pl.ds(row, ROWS), :] + (post * scaled - bar), 0.0)
                new_ref[s, t, pl.ds(row, ROWS), :] = updated
                weight = updated * scaled
                acc[t, pl.ds(row, ROWS), :] += factor * weight
                out.append(sums[t] + weight)
            return tuple(out)

        zero = jnp.zeros((ROWS, LANES), jnp.float32)
        sums = lax.fori_loop(0, tile // ROWS, row_body, (zero,) * hours)
        for t in range(hours):
            direct[me_c, s, pl.ds(t, 1), :] = jnp.sum(sums[t], axis=0, keepdims=True)
        for d in range(1, n_ctg):
            direct_copy(s, d).start()
        return carry

    lax.fori_loop(0, slots, slot_body, 0)

    columns = lax.broadcasted_iota(jnp.int32, (tile, LANES), 1)
    packed = jnp.zeros((tile, LANES), jnp.float32)
    for t in range(hours):
        packed = jnp.where(columns == t, jnp.sum(acc[t], axis=1, keepdims=True), packed)
    grad[me_l] = packed.T[:hours]
    grad_copies = []
    for d in range(1, n_line):
        copy = pltpu.make_async_remote_copy(
            src_ref=grad.at[me_l], dst_ref=grad.at[me_l],
            send_sem=grad_ssem.at[d], recv_sem=grad_rsem.at[d],
            device_id={"line": other_l(d)}, device_id_type=MESH,
        )
        copy.start()
        grad_copies.append(copy)

    for copy in map_copies:
        copy.wait_recv()

    def direct_wait(s, carry):
        for d in range(1, n_ctg):
            direct_copy(s, d).wait()
        return carry

    lax.fori_loop(0, slots, direct_wait, 0)

    for i in range(inner):
        total = jnp.zeros((hours, LANES), jnp.float32)
        for c in range(n_ctg):
            which = jnp.broadcast_to(map_recv[c, pl.ds(i, 1), :], (hours, LANES))
            found = jnp.zeros((hours, LANES), jnp.float32)
            for s in range(slots):
                found = jnp.where(which == s, direct[c, s], found)
            total = total + found
        line_ref[pl.ds(i, hours, stride=inner), :] = total * (1.0 / dual_step / outages)

    for copy in grad_copies:
        copy.wait_recv()
    total = grad[0]
    for j in range(1, n_line):
        total = total + grad[j]
    grad_ref[...] = total * (outage_scale / dual_step)

    for copy in flow_copies + map_copies + part_copies + grad_copies:
        copy.wait_send()


def per_device_fused(owned_flow, ratings, lodf_tiles, tile_map, outage_line, block_owner, multipliers):
    n_ctg = lax.axis_size("ctg")
    n_line = lax.axis_size("line")
    _, hours, piece = owned_flow.shape
    _, slots, tile, _ = lodf_tiles.shape
    inner = piece // tile
    outages = outage_line.shape[0] * n_ctg
    f32, bf16, i32 = jnp.float32, jnp.bfloat16, jnp.int32
    dma = pltpu.SemaphoreType.DMA
    vmem = pl.BlockSpec(memory_space=pltpu.VMEM)
    hbm = pl.BlockSpec(memory_space=pltpu.HBM)
    updated, line_gradient, outage_gradient = pl.pallas_call(
        functools.partial(kernel, n_ctg, n_line, outages),
        out_shape=(
            jax.ShapeDtypeStruct((slots, hours, tile, tile), f32),
            jax.ShapeDtypeStruct((hours * inner, tile), f32),
            jax.ShapeDtypeStruct((hours, tile), f32),
        ),
        in_specs=[hbm] * 7,
        out_specs=(vmem, vmem, vmem),
        scratch_shapes=[
            pltpu.SMEM(tile_map.shape, i32),
            pltpu.SMEM(block_owner.shape, i32),
            pltpu.VMEM((1, tile), i32),
            pltpu.VMEM((n_ctg * inner, tile), f32),
            pltpu.VMEM((slots, hours, tile, tile), f32),
            pltpu.VMEM((slots, tile, tile), bf16),
            pltpu.VMEM((slots, tile, tile), f32),
            pltpu.VMEM((n_ctg, hours * inner, tile), f32),
            pltpu.VMEM((n_ctg, piece, tile), bf16),
            pltpu.VMEM((hours, slots, tile), f32),
            pltpu.VMEM((slots, tile), f32),
            pltpu.VMEM((slots, tile), f32),
            pltpu.VMEM((hours, tile, tile), f32),
            pltpu.VMEM((hours, tile, tile), f32),
            pltpu.VMEM((n_ctg, slots, hours, tile), f32),
            pltpu.VMEM((n_ctg, inner, tile), i32),
            pltpu.VMEM((n_ctg, inner, tile), i32),
            pltpu.VMEM((n_line, hours, tile), f32),
            pltpu.VMEM((n_line, hours, tile), f32),
            dma((4,)), dma((slots,)), dma, dma,
            dma((n_ctg,)), dma((n_ctg,)), dma((n_ctg,)), dma((n_ctg,)),
            dma((n_line,)), dma((n_line,)),
            dma((slots, n_ctg)), dma((slots, n_ctg)),
            dma((n_line,)), dma((n_line,)),
        ],
        compiler_params=pltpu.CompilerParams(
            collective_id=0, has_side_effects=True, vmem_limit_bytes=40 * 1024 * 1024
        ),
        name="dual_step",
    )(
        *(
            pltpu.with_memory_space_constraint(x, pltpu.HBM)
            for x in (
                tile_map, block_owner, outage_line.reshape(1, tile),
                ratings.reshape(n_ctg * inner, tile), owned_flow.reshape(hours * inner, tile),
                lodf_tiles, multipliers,
            )
        )
    )
    return updated[None], line_gradient.reshape(1, hours, piece), outage_gradient


def per_device(owned_flow, ratings, lodf_tiles, tile_map, outage_line, block_owner, multipliers):
    n_ctg = lax.axis_size("ctg")
    tile = lodf_tiles.shape[-1]
    whole = (
        tile == LANES
        and owned_flow.shape[1] <= 16
        and owned_flow.shape[2] % tile == 0
        and outage_line.shape[0] == tile
        and lodf_tiles.shape[0] == 1
        and n_ctg <= 4
    )
    form = per_device_fused if whole else per_device_general
    return form(owned_flow, ratings, lodf_tiles, tile_map, outage_line, block_owner, multipliers)


def solution(mesh):
    placed = (
        P("line", "grp", "ctg"),
        P("line"),
        P("ctg", "line", None, None),
        P("ctg", "line"),
        P("ctg"),
        P(),
        P("ctg", "line", "grp", None, None),
    )
    return jax.shard_map(
        per_device,
        mesh=mesh,
        in_specs=placed,
        out_specs=(P("ctg", "line", "grp", None, None), P("line", "grp", "ctg"), P("grp", "ctg")),
        check_vma=False,
    )
```

```python
import functools

import jax
import jax.numpy as jnp
from jax import lax
from jax.experimental import pallas as pl
from jax.experimental.pallas import tpu as pltpu
from jax.sharding import PartitionSpec as P

dual_step = 0.5
outage_scale = 0.0625
MESH = pl.DeviceIdType.MESH
LANES = 128
ROWS = 8


def tile_step(tiles, slot_map, flow_rows, rating_rows, outage_flow, multipliers):
    slots = tiles.shape[0]
    match = (slot_map[:, None] == jnp.arange(slots, dtype=jnp.int32)[None, :]).astype(jnp.float32)
    slot_flow = jnp.einsum("bs,hbl->shl", match, flow_rows, precision=lax.Precision.HIGHEST)
    slot_rating = jnp.einsum("bs,bl->sl", match, rating_rows, precision=lax.Precision.HIGHEST)
    present = jnp.sum(match, axis=0)
    safe_rating = slot_rating + (1.0 - present)[:, None]
    inverse = 1.0 / (safe_rating * safe_rating)
    lodf = tiles.astype(jnp.float32)
    post = slot_flow[:, :, None, :] + lodf[:, None, :, :] * outage_flow[None, :, :, None]
    raised = multipliers + dual_step * (post * post * inverse[:, None, None, :] - 1.0)
    updated = jnp.maximum(raised, 0.0) * present[:, None, None, None]
    weight = updated * post * inverse[:, None, None, :]
    direct = jnp.sum(weight, axis=2)
    line_part = jnp.einsum("bs,shl->hbl", match, direct, precision=lax.Precision.HIGHEST)
    outage_part = jnp.sum(lodf[:, None, :, :] * weight, axis=(0, 3))
    return (updated, line_part, outage_part)


def per_device_general(owned_flow, ratings, lodf_tiles, tile_map, outage_line, block_owner, multipliers):
    hours = owned_flow.shape[1]
    piece = owned_flow.shape[2]
    ctg_count = lax.axis_size("ctg")
    line_count = lax.axis_size("line")
    shard_lines = ratings.shape[0]
    tile = lodf_tiles.shape[-1]
    kblocks = lodf_tiles.shape[0]
    outages = outage_line.shape[0] * ctg_count
    inverse_owner = (
        jnp.zeros_like(block_owner).at[block_owner].set(jnp.arange(ctg_count, dtype=jnp.int32))
    )
    gathered = lax.all_gather(owned_flow, ("ctg", "line"), axis=0, tiled=True)
    shaped = jnp.take(gathered.reshape(ctg_count, line_count, hours, piece), inverse_owner, axis=0)
    every_flow = shaped.transpose(2, 1, 0, 3).reshape(hours, line_count * shard_lines)
    shard_flow = lax.dynamic_slice_in_dim(
        every_flow, lax.axis_index("line") * shard_lines, shard_lines, 1
    )
    outage_flow = jnp.take(every_flow, outage_line, axis=1)
    flow_rows = shard_flow.reshape(hours, shard_lines // tile, tile)
    rating_rows = ratings.reshape(shard_lines // tile, tile)
    outage_blocks = outage_flow.reshape(hours, kblocks, tile).transpose(1, 0, 2)
    updated, line_part, outage_part = jax.vmap(tile_step, in_axes=(0, 0, None, None, 0, 0))(
        lodf_tiles, tile_map, flow_rows, rating_rows, outage_blocks, multipliers
    )
    line_sum = jnp.sum(line_part, axis=0).reshape(hours, shard_lines)
    line_gradient = (
        lax.psum_scatter(
            line_sum.reshape(1, hours, shard_lines), "ctg", scatter_dimension=2, tiled=True
        )
        / outages
    )
    outage_local = outage_part.transpose(1, 0, 2).reshape(hours, kblocks * tile)
    outage_gradient = lax.psum(outage_local, "line") * outage_scale
    return (updated, line_gradient, outage_gradient)


def kernel(
    n_ctg, n_line, outages, hours,
    map_hbm, owner_hbm, outage_hbm, rating_hbm, own_hbm, lodf_hbm, mult_hbm,
    new_ref, line_ref, grad_ref,
    map_ref, owner_ref, outage_ref, rating_ref,
    mult, lodf16, lodf, flows, onehot, slot_flow, slot_half, slot_bar, spread, acc, direct,
    map_send, map_recv, part, grad,
    small_sem, mult_sem, lodf_sem, own_sem, flow_ssem, flow_rsem, map_ssem, map_rsem,
    part_ssem, part_rsem, dir_ssem, dir_rsem, grad_ssem, grad_rsem,
):
    slots, _, tile, _ = mult.shape
    groups, span = part.shape[1:3]
    inner = flows.shape[1] // hours
    piece = inner * tile
    me_c = lax.axis_index("ctg")
    me_l = lax.axis_index("line")

    def other_c(d):
        return lax.rem(me_c + d, n_ctg)

    def other_l(d):
        return lax.rem(me_l + d, n_line)

    def to_ctg(src, dst, ssem, rsem, d):
        return pltpu.make_async_remote_copy(
            src_ref=src, dst_ref=dst, send_sem=ssem, recv_sem=rsem,
            device_id={"ctg": other_c(d)}, device_id_type=MESH,
        )

    def to_line(src, dst, ssem, rsem, d):
        return pltpu.make_async_remote_copy(
            src_ref=src, dst_ref=dst, send_sem=ssem, recv_sem=rsem,
            device_id={"line": other_l(d)}, device_id_type=MESH,
        )

    barrier = pltpu.get_barrier_semaphore()
    for d in range(1, n_ctg):
        pl.semaphore_signal(barrier, inc=1, device_id={"ctg": other_c(d)}, device_id_type=MESH)
    for d in range(1, n_line):
        pl.semaphore_signal(barrier, inc=1, device_id={"line": other_l(d)}, device_id_type=MESH)

    own_copy = pltpu.make_async_copy(own_hbm, flows.at[me_c], own_sem)
    own_copy.start()
    small_copies = [
        pltpu.make_async_copy(src, dst, small_sem.at[i])
        for i, (src, dst) in enumerate(
            ((map_hbm, map_ref), (owner_hbm, owner_ref), (outage_hbm, outage_ref), (rating_hbm, rating_ref))
        )
    ]
    for copy in small_copies:
        copy.start()
    lodf_copy = pltpu.make_async_copy(lodf_hbm.at[0], lodf16, lodf_sem)
    lodf_copy.start()
    for s in range(slots):
        pltpu.make_async_copy(mult_hbm.at[0, s], mult.at[s], mult_sem.at[s]).start()

    for copy in small_copies:
        copy.wait()
    for q in range(n_ctg):
        for i in range(inner):
            map_send[q, pl.ds(i, 1), :] = jnp.full((1, LANES), map_ref[0, q * inner + i], jnp.int32)
    own_copy.wait()
    pl.semaphore_wait(barrier, n_ctg - 1 + n_line - 1)

    far = (2, 1, 3) if n_ctg == 4 else tuple(range(1, n_ctg))
    flow_copies = []
    for g in range(groups):
        rows = flows.at[me_c, pl.ds(g * span * inner, span * inner)]
        copies = [to_ctg(rows, rows, flow_ssem.at[g, d], flow_rsem.at[g, d], d) for d in far]
        for copy in copies:
            copy.start()
        flow_copies.append(copies)
    map_copies = []
    for d in range(1, n_ctg):
        copy = to_ctg(map_send.at[other_c(d)], map_recv.at[me_c], map_ssem.at[d], map_rsem.at[d], d)
        copy.start()
        map_copies.append(copy)
    map_recv[me_c] = map_send[me_c]

    rows_iota = lax.broadcasted_iota(jnp.int32, (tile, LANES), 0)
    for c in range(n_ctg):
        base = (me_l * n_ctg + owner_ref[c]) * piece
        wanted = jnp.broadcast_to(outage_ref[...] - base, (tile, LANES))

        def hot_body(b, carry, c=c, wanted=wanted):
            row = pl.multiple_of(b * tile, tile)
            hit = (rows_iota + row) == wanted
            onehot[c, pl.ds(row, tile), :] = jnp.where(hit, 1.0, 0.0).astype(jnp.bfloat16)
            return carry

        lax.fori_loop(0, inner, hot_body, 0)

    slot_iota = lax.broadcasted_iota(jnp.int32, (slots, LANES), 0)
    rating = jnp.ones((slots, LANES), jnp.float32)
    there = jnp.zeros((slots, LANES), jnp.float32)
    for b in range(n_ctg * inner):
        hit = slot_iota == map_ref[0, b]
        rating = jnp.where(hit, jnp.broadcast_to(rating_ref[pl.ds(b, 1), :], (slots, LANES)), rating)
        there = jnp.where(hit, 1.0, there)
    slot_half[...] = there * (dual_step / (rating * rating))
    slot_bar[...] = jnp.where(there > 0.0, dual_step, 1e30)

    lodf_copy.wait()

    def lodf_body(s, carry):
        lodf[s] = lodf16[s].astype(jnp.float32)
        return carry

    lax.fori_loop(0, slots, lodf_body, 0)
    acc[...] = jnp.zeros_like(acc)

    block_at = []
    for c in range(n_ctg):
        for i in range(inner):
            block = jnp.int32(-1)
            for q in range(n_ctg):
                block = jnp.where(owner_ref[c] == q, map_ref[0, q * inner + i], block)
            block_at.append(block)

    def pick(c, g):
        value = jnp.concatenate(
            [flows[c, pl.ds(g * span * inner + i, span, stride=inner), :] for i in range(inner)], axis=1
        )
        high = value.astype(jnp.bfloat16).astype(jnp.float32)
        rest = value - high
        middle = rest.astype(jnp.bfloat16).astype(jnp.float32)
        low = rest - middle
        parts = jnp.concatenate([high, middle, low, jnp.zeros_like(low)], axis=0).astype(jnp.bfloat16)
        total = jnp.dot(parts, onehot[c], preferred_element_type=jnp.float32)
        return total[:span] + total[span : 2 * span] + total[2 * span : 3 * span]

    def gather(g):
        for copy in flow_copies[g]:
            copy.wait_recv()
        picked = pick(0, g)
        for c in range(1, n_ctg):
            picked = picked + pick(c, g)
        part[me_l, g] = picked
        mine = part.at[me_l, g]
        copies = [
            to_line(mine, mine, part_ssem.at[g, d], part_rsem.at[g, d], d) for d in range(1, n_line)
        ]
        for copy in copies:
            copy.start()
        found = [jnp.zeros((slots, LANES), jnp.float32)] * span
        for c in range(n_ctg):
            for i in range(inner):
                hit = slot_iota == block_at[c * inner + i]
                for t in range(span):
                    row = flows[c, pl.ds((g * span + t) * inner + i, 1), :]
                    found[t] = jnp.where(hit, jnp.broadcast_to(row, (slots, LANES)), found[t])
        for t in range(span):
            slot_flow[g * span + t] = found[t]
        return copies

    def update(g, part_copies):
        for copy in part_copies:
            copy.wait_recv()
        outage = part[0, g]
        for j in range(1, n_line):
            outage = outage + part[j, g]
        turned = jnp.concatenate([outage, jnp.zeros((ROWS - span, LANES), jnp.float32)], axis=0).T
        for t in range(span):
            spread[t] = jnp.broadcast_to(turned[:, t : t + 1], (tile, LANES))
        first = g * span

        def pair_body(p, carry):
            pair = [2 * p, 2 * p + 1]
            if g == 0:
                for s in pair:
                    pltpu.make_async_copy(mult_hbm.at[0, s], mult.at[s], mult_sem.at[s]).wait()

            def lines(ref, s):
                return jnp.broadcast_to(ref[pl.ds(s, 1), :], (ROWS, LANES))

            half = [lines(slot_half, s) for s in pair]
            bar = [lines(slot_bar, s) for s in pair]
            base = [[lines(slot_flow.at[first + t], s) for t in range(span)] for s in pair]

            def row_body(k, sums):
                row = pl.multiple_of(k * ROWS, ROWS)
                rows = pl.ds(row, ROWS)
                factor = [lodf[s, rows, :] for s in pair]
                out = [None] * (2 * span)
                for t in range(span):
                    flow = spread[t, rows, :]
                    total = acc[first + t, rows, :]
                    for e, s in enumerate(pair):
                        post = base[e][t] + factor[e] * flow
                        scaled = post * half[e]
                        updated = jnp.maximum(
                            mult[s, first + t, rows, :] + (post * scaled - bar[e]), 0.0
                        )
                        new_ref[s, first + t, rows, :] = updated
                        weight = updated * scaled
                        total = total + factor[e] * weight
                        out[e * span + t] = sums[e * span + t] + weight
                    acc[first + t, rows, :] = total
                return tuple(out)

            zero = jnp.zeros((ROWS, LANES), jnp.float32)
            sums = lax.fori_loop(0, tile // ROWS, row_body, (zero,) * (2 * span), unroll=2)
            for e, s in enumerate(pair):
                for t in range(span):
                    direct[me_c, g, pl.ds(s * span + t, 1), :] = jnp.sum(
                        sums[e * span + t], axis=0, keepdims=True
                    )
            return carry

        lax.fori_loop(0, slots // 2, pair_body, 0)
        mine = direct.at[me_c, g]
        copies = [to_ctg(mine, mine, dir_ssem.at[g, d], dir_rsem.at[g, d], d) for d in far]
        for copy in copies:
            copy.start()
        columns = lax.broadcasted_iota(jnp.int32, (tile, LANES), 1)
        packed = jnp.zeros((tile, LANES), jnp.float32)
        for t in range(span):
            packed = jnp.where(columns == t, jnp.sum(acc[first + t], axis=1, keepdims=True), packed)
        grad[me_l, g] = packed.T[:span]
        return copies

    def combine(g, direct_copies):
        for copy in direct_copies:
            copy.wait_recv()
        for t in range(span):
            total = jnp.zeros((inner, LANES), jnp.float32)
            for c in range(n_ctg):
                which = map_recv[c]
                for s in range(slots):
                    row = direct[c, g, pl.ds(s * span + t, 1), :]
                    total = total + jnp.where(which == s, jnp.broadcast_to(row, (inner, LANES)), 0.0)
            line_ref[pl.ds((g * span + t) * inner, inner), :] = total * (1.0 / dual_step / outages)

    part_copies, direct_copies = [], []
    for g in range(groups):
        part_copies.append(gather(g))
        if g >= 1:
            direct_copies.append(update(g - 1, part_copies[g - 1]))
    direct_copies.append(update(groups - 1, part_copies[groups - 1]))

    mine = grad.at[me_l]
    grad_copies = [to_line(mine, mine, grad_ssem.at[d], grad_rsem.at[d], d) for d in range(1, n_line)]
    for copy in grad_copies:
        copy.start()

    for copy in map_copies:
        copy.wait_recv()
    for g in range(groups):
        combine(g, direct_copies[g])

    for copy in grad_copies:
        copy.wait_recv()
    for g in range(groups):
        total = grad[0, g]
        for j in range(1, n_line):
            total = total + grad[j, g]
        grad_ref[pl.ds(g * span, span), :] = total * (outage_scale / dual_step)

    for copies in flow_copies + part_copies + direct_copies + [map_copies, grad_copies]:
        for copy in copies:
            copy.wait_send()


def write_out(new_vmem, line_vmem, grad_vmem, new_hbm, line_hbm, grad_hbm, sems):
    slots = new_vmem.shape[0]
    copies = [pltpu.make_async_copy(new_vmem.at[s], new_hbm.at[s], sems.at[s]) for s in range(slots)]
    copies.append(pltpu.make_async_copy(line_vmem, line_hbm, sems.at[slots]))
    copies.append(pltpu.make_async_copy(grad_vmem, grad_hbm, sems.at[slots + 1]))
    for copy in copies:
        copy.start()
    for copy in copies:
        copy.wait()


def per_device_fused(owned_flow, ratings, lodf_tiles, tile_map, outage_line, block_owner, multipliers):
    n_ctg = lax.axis_size("ctg")
    n_line = lax.axis_size("line")
    _, hours, piece = owned_flow.shape
    _, slots, tile, _ = lodf_tiles.shape
    inner = piece // tile
    outages = outage_line.shape[0] * n_ctg
    span = 4
    groups = hours // span
    f32, bf16, i32 = jnp.float32, jnp.bfloat16, jnp.int32
    dma = pltpu.SemaphoreType.DMA
    vmem = pl.BlockSpec(memory_space=pltpu.VMEM)
    hbm = pl.BlockSpec(memory_space=pltpu.HBM)
    anywhere = pl.BlockSpec(memory_space=pl.ANY)
    shapes = (
        jax.ShapeDtypeStruct((slots, hours, tile, tile), f32),
        jax.ShapeDtypeStruct((hours * inner, tile), f32),
        jax.ShapeDtypeStruct((hours, tile), f32),
    )
    results = pl.pallas_call(
        functools.partial(kernel, n_ctg, n_line, outages, hours),
        out_shape=shapes,
        in_specs=[hbm] * 7,
        out_specs=(vmem, vmem, vmem),
        scratch_shapes=[
            pltpu.SMEM(tile_map.shape, i32),
            pltpu.SMEM(block_owner.shape, i32),
            pltpu.VMEM((1, tile), i32),
            pltpu.VMEM((n_ctg * inner, tile), f32),
            pltpu.VMEM((slots, hours, tile, tile), f32),
            pltpu.VMEM((slots, tile, tile), bf16),
            pltpu.VMEM((slots, tile, tile), f32),
            pltpu.VMEM((n_ctg, hours * inner, tile), f32),
            pltpu.VMEM((n_ctg, piece, tile), bf16),
            pltpu.VMEM((hours, slots, tile), f32),
            pltpu.VMEM((slots, tile), f32),
            pltpu.VMEM((slots, tile), f32),
            pltpu.VMEM((span, tile, tile), f32),
            pltpu.VMEM((hours, tile, tile), f32),
            pltpu.VMEM((n_ctg, groups, slots * span, tile), f32),
            pltpu.VMEM((n_ctg, inner, tile), i32),
            pltpu.VMEM((n_ctg, inner, tile), i32),
            pltpu.VMEM((n_line, groups, span, tile), f32),
            pltpu.VMEM((n_line, groups, span, tile), f32),
            dma((4,)), dma((slots,)), dma, dma,
            dma((groups, n_ctg)), dma((groups, n_ctg)), dma((n_ctg,)), dma((n_ctg,)),
            dma((groups, n_line)), dma((groups, n_line)),
            dma((groups, n_ctg)), dma((groups, n_ctg)),
            dma((n_line,)), dma((n_line,)),
        ],
        compiler_params=pltpu.CompilerParams(
            collective_id=0, has_side_effects=True, vmem_limit_bytes=40 * 1024 * 1024
        ),
        name="dual_step",
    )(
        *(
            pltpu.with_memory_space_constraint(x, pltpu.HBM)
            for x in (
                tile_map, block_owner, outage_line.reshape(1, tile),
                ratings.reshape(n_ctg * inner, tile), owned_flow.reshape(hours * inner, tile),
                lodf_tiles, multipliers,
            )
        )
    )
    updated, line_gradient, outage_gradient = pl.pallas_call(
        write_out,
        out_shape=shapes,
        in_specs=[anywhere] * 3,
        out_specs=(anywhere,) * 3,
        scratch_shapes=[dma((slots + 2,))],
        name="write_out",
    )(*results)
    return updated[None], line_gradient.reshape(1, hours, piece), outage_gradient


def per_device(owned_flow, ratings, lodf_tiles, tile_map, outage_line, block_owner, multipliers):
    n_ctg = lax.axis_size("ctg")
    tile = lodf_tiles.shape[-1]
    whole = (
        tile == LANES
        and owned_flow.shape[1] % 4 == 0
        and lodf_tiles.shape[1] == 8
        and owned_flow.shape[2] % tile == 0
        and outage_line.shape[0] == tile
        and lodf_tiles.shape[0] == 1
        and n_ctg <= 4
    )
    form = per_device_fused if whole else per_device_general
    return form(owned_flow, ratings, lodf_tiles, tile_map, outage_line, block_owner, multipliers)


def solution(mesh):
    placed = (
        P("line", "grp", "ctg"),
        P("line"),
        P("ctg", "line", None, None),
        P("ctg", "line"),
        P("ctg"),
        P(),
        P("ctg", "line", "grp", None, None),
    )
    return jax.shard_map(
        per_device,
        mesh=mesh,
        in_specs=placed,
        out_specs=(P("ctg", "line", "grp", None, None), P("line", "grp", "ctg"), P("grp", "ctg")),
        check_vma=False,
    )
```

```python
import functools

import jax
import jax.numpy as jnp
from jax import lax
from jax.experimental import pallas as pl
from jax.experimental.pallas import tpu as pltpu
from jax.sharding import PartitionSpec as P

dual_step = 0.5
outage_scale = 0.0625
MESH = pl.DeviceIdType.MESH
LANES = 128
ROWS = 8


def tile_step(tiles, slot_map, flow_rows, rating_rows, outage_flow, multipliers):
    slots = tiles.shape[0]
    match = (slot_map[:, None] == jnp.arange(slots, dtype=jnp.int32)[None, :]).astype(jnp.float32)
    slot_flow = jnp.einsum("bs,hbl->shl", match, flow_rows, precision=lax.Precision.HIGHEST)
    slot_rating = jnp.einsum("bs,bl->sl", match, rating_rows, precision=lax.Precision.HIGHEST)
    present = jnp.sum(match, axis=0)
    safe_rating = slot_rating + (1.0 - present)[:, None]
    inverse = 1.0 / (safe_rating * safe_rating)
    lodf = tiles.astype(jnp.float32)
    post = slot_flow[:, :, None, :] + lodf[:, None, :, :] * outage_flow[None, :, :, None]
    raised = multipliers + dual_step * (post * post * inverse[:, None, None, :] - 1.0)
    updated = jnp.maximum(raised, 0.0) * present[:, None, None, None]
    weight = updated * post * inverse[:, None, None, :]
    direct = jnp.sum(weight, axis=2)
    line_part = jnp.einsum("bs,shl->hbl", match, direct, precision=lax.Precision.HIGHEST)
    outage_part = jnp.sum(lodf[:, None, :, :] * weight, axis=(0, 3))
    return (updated, line_part, outage_part)


def per_device_general(owned_flow, ratings, lodf_tiles, tile_map, outage_line, block_owner, multipliers):
    hours = owned_flow.shape[1]
    piece = owned_flow.shape[2]
    ctg_count = lax.axis_size("ctg")
    line_count = lax.axis_size("line")
    shard_lines = ratings.shape[0]
    tile = lodf_tiles.shape[-1]
    kblocks = lodf_tiles.shape[0]
    outages = outage_line.shape[0] * ctg_count
    inverse_owner = (
        jnp.zeros_like(block_owner).at[block_owner].set(jnp.arange(ctg_count, dtype=jnp.int32))
    )
    gathered = lax.all_gather(owned_flow, ("ctg", "line"), axis=0, tiled=True)
    shaped = jnp.take(gathered.reshape(ctg_count, line_count, hours, piece), inverse_owner, axis=0)
    every_flow = shaped.transpose(2, 1, 0, 3).reshape(hours, line_count * shard_lines)
    shard_flow = lax.dynamic_slice_in_dim(
        every_flow, lax.axis_index("line") * shard_lines, shard_lines, 1
    )
    outage_flow = jnp.take(every_flow, outage_line, axis=1)
    flow_rows = shard_flow.reshape(hours, shard_lines // tile, tile)
    rating_rows = ratings.reshape(shard_lines // tile, tile)
    outage_blocks = outage_flow.reshape(hours, kblocks, tile).transpose(1, 0, 2)
    updated, line_part, outage_part = jax.vmap(tile_step, in_axes=(0, 0, None, None, 0, 0))(
        lodf_tiles, tile_map, flow_rows, rating_rows, outage_blocks, multipliers
    )
    line_sum = jnp.sum(line_part, axis=0).reshape(hours, shard_lines)
    line_gradient = (
        lax.psum_scatter(
            line_sum.reshape(1, hours, shard_lines), "ctg", scatter_dimension=2, tiled=True
        )
        / outages
    )
    outage_local = outage_part.transpose(1, 0, 2).reshape(hours, kblocks * tile)
    outage_gradient = lax.psum(outage_local, "line") * outage_scale
    return (updated, line_gradient, outage_gradient)


def kernel(
    n_ctg, n_line, outages, hours,
    map_hbm, owner_hbm, outage_hbm, rating_hbm, own_hbm, lodf_hbm, mult_hbm,
    new_ref, line_ref, grad_ref,
    map_ref, owner_ref, outage_ref, rating_ref,
    mult, lodf16, lodf, flows, onehot, slot_flow, slot_half, slot_bar, spread, acc, direct,
    map_send, map_recv, part, grad,
    small_sem, mult_sem, lodf_sem, own_sem, flow_ssem, flow_rsem, map_ssem, map_rsem,
    part_ssem, part_rsem, dir_ssem, dir_rsem, grad_ssem, grad_rsem,
):
    slots, _, tile, _ = mult.shape
    groups, span = part.shape[1:3]
    inner = flows.shape[1] // hours
    piece = inner * tile
    me_c = lax.axis_index("ctg")
    me_l = lax.axis_index("line")

    def other_c(d):
        return lax.rem(me_c + d, n_ctg)

    def other_l(d):
        return lax.rem(me_l + d, n_line)

    def to_ctg(src, dst, ssem, rsem, d):
        return pltpu.make_async_remote_copy(
            src_ref=src, dst_ref=dst, send_sem=ssem, recv_sem=rsem,
            device_id={"ctg": other_c(d)}, device_id_type=MESH,
        )

    def to_line(src, dst, ssem, rsem, d):
        return pltpu.make_async_remote_copy(
            src_ref=src, dst_ref=dst, send_sem=ssem, recv_sem=rsem,
            device_id={"line": other_l(d)}, device_id_type=MESH,
        )

    barrier = pltpu.get_barrier_semaphore()
    for d in range(1, n_ctg):
        pl.semaphore_signal(barrier, inc=1, device_id={"ctg": other_c(d)}, device_id_type=MESH)
    for d in range(1, n_line):
        pl.semaphore_signal(barrier, inc=1, device_id={"line": other_l(d)}, device_id_type=MESH)

    own_copy = pltpu.make_async_copy(own_hbm, flows.at[me_c], own_sem)
    own_copy.start()
    small_copies = [
        pltpu.make_async_copy(src, dst, small_sem.at[i])
        for i, (src, dst) in enumerate(
            ((map_hbm, map_ref), (owner_hbm, owner_ref), (outage_hbm, outage_ref), (rating_hbm, rating_ref))
        )
    ]
    for copy in small_copies:
        copy.start()
    lodf_copy = pltpu.make_async_copy(lodf_hbm.at[0], lodf16, lodf_sem)
    lodf_copy.start()
    for s in range(slots):
        pltpu.make_async_copy(mult_hbm.at[0, s], mult.at[s], mult_sem.at[s]).start()

    for copy in small_copies:
        copy.wait()
    for q in range(n_ctg):
        for i in range(inner):
            map_send[q, pl.ds(i, 1), :] = jnp.full((1, LANES), map_ref[0, q * inner + i], jnp.int32)
    own_copy.wait()
    pl.semaphore_wait(barrier, n_ctg - 1 + n_line - 1)

    far = (2, 1, 3) if n_ctg == 4 else tuple(range(1, n_ctg))
    flow_copies = []
    for g in range(groups):
        rows = flows.at[me_c, pl.ds(g * span * inner, span * inner)]
        copies = [to_ctg(rows, rows, flow_ssem.at[g, d], flow_rsem.at[g, d], d) for d in far]
        for copy in copies:
            copy.start()
        flow_copies.append(copies)
    map_copies = []
    for d in range(1, n_ctg):
        copy = to_ctg(map_send.at[other_c(d)], map_recv.at[me_c], map_ssem.at[d], map_rsem.at[d], d)
        copy.start()
        map_copies.append(copy)
    map_recv[me_c] = map_send[me_c]

    rows_iota = lax.broadcasted_iota(jnp.int32, (tile, LANES), 0)
    for c in range(n_ctg):
        base = (me_l * n_ctg + owner_ref[c]) * piece
        wanted = jnp.broadcast_to(outage_ref[...] - base, (tile, LANES))

        def hot_body(b, carry, c=c, wanted=wanted):
            row = pl.multiple_of(b * tile, tile)
            hit = (rows_iota + row) == wanted
            onehot[c, pl.ds(row, tile), :] = jnp.where(hit, 1.0, 0.0).astype(jnp.bfloat16)
            return carry

        lax.fori_loop(0, inner, hot_body, 0)

    slot_iota = lax.broadcasted_iota(jnp.int32, (slots, LANES), 0)
    rating = jnp.ones((slots, LANES), jnp.float32)
    there = jnp.zeros((slots, LANES), jnp.float32)
    for b in range(n_ctg * inner):
        hit = slot_iota == map_ref[0, b]
        rating = jnp.where(hit, jnp.broadcast_to(rating_ref[pl.ds(b, 1), :], (slots, LANES)), rating)
        there = jnp.where(hit, 1.0, there)
    slot_half[...] = there * (dual_step / (rating * rating))
    slot_bar[...] = jnp.where(there > 0.0, dual_step, 1e30)

    lodf_copy.wait()

    def lodf_body(s, carry):
        lodf[s] = lodf16[s].astype(jnp.float32)
        return carry

    lax.fori_loop(0, slots, lodf_body, 0)
    acc[...] = jnp.zeros_like(acc)

    block_at = []
    for c in range(n_ctg):
        for i in range(inner):
            block = jnp.int32(-1)
            for q in range(n_ctg):
                block = jnp.where(owner_ref[c] == q, map_ref[0, q * inner + i], block)
            block_at.append(block)

    def pick(c, g):
        value = jnp.concatenate(
            [flows[c, pl.ds(g * span * inner + i, span, stride=inner), :] for i in range(inner)], axis=1
        )
        high = value.astype(jnp.bfloat16).astype(jnp.float32)
        rest = value - high
        middle = rest.astype(jnp.bfloat16).astype(jnp.float32)
        low = rest - middle
        parts = jnp.concatenate([high, middle, low, jnp.zeros_like(low)], axis=0).astype(jnp.bfloat16)
        total = jnp.dot(parts, onehot[c], preferred_element_type=jnp.float32)
        return total[:span] + total[span : 2 * span] + total[2 * span : 3 * span]

    def gather(g):
        for copy in flow_copies[g]:
            copy.wait_recv()
        picked = pick(0, g)
        for c in range(1, n_ctg):
            picked = picked + pick(c, g)
        part[me_l, g] = picked
        mine = part.at[me_l, g]
        copies = [
            to_line(mine, mine, part_ssem.at[g, d], part_rsem.at[g, d], d) for d in range(1, n_line)
        ]
        for copy in copies:
            copy.start()
        found = [jnp.zeros((slots, LANES), jnp.float32)] * span
        for c in range(n_ctg):
            for i in range(inner):
                hit = slot_iota == block_at[c * inner + i]
                for t in range(span):
                    row = flows[c, pl.ds((g * span + t) * inner + i, 1), :]
                    found[t] = jnp.where(hit, jnp.broadcast_to(row, (slots, LANES)), found[t])
        for t in range(span):
            slot_flow[g * span + t] = found[t]
        return copies

    def update(g, part_copies):
        for copy in part_copies:
            copy.wait_recv()
        outage = part[0, g]
        for j in range(1, n_line):
            outage = outage + part[j, g]
        turned = jnp.concatenate([outage, jnp.zeros((ROWS - span, LANES), jnp.float32)], axis=0).T
        for t in range(span):
            spread[t] = jnp.broadcast_to(turned[:, t : t + 1], (tile, LANES))
        first = g * span

        def pair_body(p, carry):
            pair = [2 * p, 2 * p + 1]
            if g == 0:
                for s in pair:
                    pltpu.make_async_copy(mult_hbm.at[0, s], mult.at[s], mult_sem.at[s]).wait()

            def lines(ref, s):
                return jnp.broadcast_to(ref[pl.ds(s, 1), :], (ROWS, LANES))

            half = [lines(slot_half, s) for s in pair]
            bar = [lines(slot_bar, s) for s in pair]
            base = [[lines(slot_flow.at[first + t], s) for t in range(span)] for s in pair]

            def row_body(k, sums):
                row = pl.multiple_of(k * ROWS, ROWS)
                rows = pl.ds(row, ROWS)
                factor = [lodf[s, rows, :] for s in pair]
                out = [None] * (2 * span)
                for t in range(span):
                    flow = spread[t, rows, :]
                    total = acc[first + t, rows, :]
                    for e, s in enumerate(pair):
                        post = base[e][t] + factor[e] * flow
                        scaled = post * half[e]
                        updated = jnp.maximum(
                            mult[s, first + t, rows, :] + (post * scaled - bar[e]), 0.0
                        )
                        new_ref[s, first + t, rows, :] = updated
                        weight = updated * scaled
                        total = total + factor[e] * weight
                        out[e * span + t] = sums[e * span + t] + weight
                    acc[first + t, rows, :] = total
                return tuple(out)

            zero = jnp.zeros((ROWS, LANES), jnp.float32)
            sums = lax.fori_loop(0, tile // ROWS, row_body, (zero,) * (2 * span), unroll=2)
            for e, s in enumerate(pair):
                for t in range(span):
                    direct[me_c, g, pl.ds(s * span + t, 1), :] = jnp.sum(
                        sums[e * span + t], axis=0, keepdims=True
                    )
            return carry

        lax.fori_loop(0, slots // 2, pair_body, 0)
        mine = direct.at[me_c, g]
        copies = [to_ctg(mine, mine, dir_ssem.at[g, d], dir_rsem.at[g, d], d) for d in far]
        for copy in copies:
            copy.start()
        columns = lax.broadcasted_iota(jnp.int32, (tile, LANES), 1)
        packed = jnp.zeros((tile, LANES), jnp.float32)
        for t in range(span):
            packed = jnp.where(columns == t, jnp.sum(acc[first + t], axis=1, keepdims=True), packed)
        grad[me_l, g] = packed.T[:span]
        return copies

    def combine(g, direct_copies):
        for copy in direct_copies:
            copy.wait_recv()
        for t in range(span):
            total = jnp.zeros((inner, LANES), jnp.float32)
            for c in range(n_ctg):
                which = map_recv[c]
                for s in range(slots):
                    row = direct[c, g, pl.ds(s * span + t, 1), :]
                    total = total + jnp.where(which == s, jnp.broadcast_to(row, (inner, LANES)), 0.0)
            line_ref[pl.ds((g * span + t) * inner, inner), :] = total * (1.0 / dual_step / outages)

    part_copies, direct_copies = [], []
    for g in range(groups):
        part_copies.append(gather(g))
        if g >= 1:
            direct_copies.append(update(g - 1, part_copies[g - 1]))
    direct_copies.append(update(groups - 1, part_copies[groups - 1]))

    mine = grad.at[me_l]
    grad_copies = [to_line(mine, mine, grad_ssem.at[d], grad_rsem.at[d], d) for d in range(1, n_line)]
    for copy in grad_copies:
        copy.start()

    for copy in map_copies:
        copy.wait_recv()
    for g in range(groups):
        combine(g, direct_copies[g])

    for copy in grad_copies:
        copy.wait_recv()
    for g in range(groups):
        total = grad[0, g]
        for j in range(1, n_line):
            total = total + grad[j, g]
        grad_ref[pl.ds(g * span, span), :] = total * (outage_scale / dual_step)

    for copies in flow_copies + part_copies + direct_copies + [map_copies, grad_copies]:
        for copy in copies:
            copy.wait_send()


def write_out(new_vmem, line_vmem, grad_vmem, new_hbm, line_hbm, grad_hbm, sems):
    slots = new_vmem.shape[0]
    copies = [pltpu.make_async_copy(new_vmem.at[s], new_hbm.at[s], sems.at[s]) for s in range(slots)]
    copies.append(pltpu.make_async_copy(line_vmem, line_hbm, sems.at[slots]))
    copies.append(pltpu.make_async_copy(grad_vmem, grad_hbm, sems.at[slots + 1]))
    for copy in copies:
        copy.start()
    for copy in copies:
        copy.wait()


def per_device_fused(owned_flow, ratings, lodf_tiles, tile_map, outage_line, block_owner, multipliers):
    n_ctg = lax.axis_size("ctg")
    n_line = lax.axis_size("line")
    _, hours, piece = owned_flow.shape
    _, slots, tile, _ = lodf_tiles.shape
    inner = piece // tile
    outages = outage_line.shape[0] * n_ctg
    span = 4
    groups = hours // span
    f32, bf16, i32 = jnp.float32, jnp.bfloat16, jnp.int32
    dma = pltpu.SemaphoreType.DMA
    vmem = pl.BlockSpec(memory_space=pltpu.VMEM)
    hbm = pl.BlockSpec(memory_space=pltpu.HBM)
    shapes = (
        jax.ShapeDtypeStruct((slots, hours, tile, tile), f32),
        jax.ShapeDtypeStruct((hours * inner, tile), f32),
        jax.ShapeDtypeStruct((hours, tile), f32),
    )
    results = pl.pallas_call(
        functools.partial(kernel, n_ctg, n_line, outages, hours),
        out_shape=shapes,
        in_specs=[hbm] * 7,
        out_specs=(vmem, vmem, vmem),
        scratch_shapes=[
            pltpu.SMEM(tile_map.shape, i32),
            pltpu.SMEM(block_owner.shape, i32),
            pltpu.VMEM((1, tile), i32),
            pltpu.VMEM((n_ctg * inner, tile), f32),
            pltpu.VMEM((slots, hours, tile, tile), f32),
            pltpu.VMEM((slots, tile, tile), bf16),
            pltpu.VMEM((slots, tile, tile), f32),
            pltpu.VMEM((n_ctg, hours * inner, tile), f32),
            pltpu.VMEM((n_ctg, piece, tile), bf16),
            pltpu.VMEM((hours, slots, tile), f32),
            pltpu.VMEM((slots, tile), f32),
            pltpu.VMEM((slots, tile), f32),
            pltpu.VMEM((span, tile, tile), f32),
            pltpu.VMEM((hours, tile, tile), f32),
            pltpu.VMEM((n_ctg, groups, slots * span, tile), f32),
            pltpu.VMEM((n_ctg, inner, tile), i32),
            pltpu.VMEM((n_ctg, inner, tile), i32),
            pltpu.VMEM((n_line, groups, span, tile), f32),
            pltpu.VMEM((n_line, groups, span, tile), f32),
            dma((4,)), dma((slots,)), dma, dma,
            dma((groups, n_ctg)), dma((groups, n_ctg)), dma((n_ctg,)), dma((n_ctg,)),
            dma((groups, n_line)), dma((groups, n_line)),
            dma((groups, n_ctg)), dma((groups, n_ctg)),
            dma((n_line,)), dma((n_line,)),
        ],
        compiler_params=pltpu.CompilerParams(
            collective_id=0, has_side_effects=True, vmem_limit_bytes=40 * 1024 * 1024
        ),
        name="dual_step",
    )(
        *(
            pltpu.with_memory_space_constraint(x, pltpu.HBM)
            for x in (
                tile_map, block_owner, outage_line.reshape(1, tile),
                ratings.reshape(n_ctg * inner, tile), owned_flow.reshape(hours * inner, tile),
                lodf_tiles, multipliers,
            )
        )
    )
    updated, line_gradient, outage_gradient = pl.pallas_call(
        write_out,
        out_shape=shapes,
        in_specs=[vmem] * 3,
        out_specs=(hbm,) * 3,
        scratch_shapes=[dma((slots + 2,))],
        compiler_params=pltpu.CompilerParams(vmem_limit_bytes=40 * 1024 * 1024),
        name="write_out",
    )(*(pltpu.with_memory_space_constraint(x, pltpu.VMEM) for x in results))
    return updated[None], line_gradient.reshape(1, hours, piece), outage_gradient


def per_device(owned_flow, ratings, lodf_tiles, tile_map, outage_line, block_owner, multipliers):
    n_ctg = lax.axis_size("ctg")
    tile = lodf_tiles.shape[-1]
    whole = (
        tile == LANES
        and owned_flow.shape[1] % 4 == 0
        and lodf_tiles.shape[1] == 8
        and owned_flow.shape[2] % tile == 0
        and outage_line.shape[0] == tile
        and lodf_tiles.shape[0] == 1
        and n_ctg <= 4
    )
    form = per_device_fused if whole else per_device_general
    return form(owned_flow, ratings, lodf_tiles, tile_map, outage_line, block_owner, multipliers)


def solution(mesh):
    placed = (
        P("line", "grp", "ctg"),
        P("line"),
        P("ctg", "line", None, None),
        P("ctg", "line"),
        P("ctg"),
        P(),
        P("ctg", "line", "grp", None, None),
    )
    return jax.shard_map(
        per_device,
        mesh=mesh,
        in_specs=placed,
        out_specs=(P("ctg", "line", "grp", None, None), P("line", "grp", "ctg"), P("grp", "ctg")),
        check_vma=False,
    )
```

```python
import functools

import jax
import jax.numpy as jnp
from jax import lax
from jax.experimental import pallas as pl
from jax.experimental.pallas import tpu as pltpu
from jax.sharding import PartitionSpec as P

dual_step = 0.5
outage_scale = 0.0625
MESH = pl.DeviceIdType.MESH
LANES = 128
ROWS = 8


def tile_step(tiles, slot_map, flow_rows, rating_rows, outage_flow, multipliers):
    slots = tiles.shape[0]
    match = (slot_map[:, None] == jnp.arange(slots, dtype=jnp.int32)[None, :]).astype(jnp.float32)
    slot_flow = jnp.einsum("bs,hbl->shl", match, flow_rows, precision=lax.Precision.HIGHEST)
    slot_rating = jnp.einsum("bs,bl->sl", match, rating_rows, precision=lax.Precision.HIGHEST)
    present = jnp.sum(match, axis=0)
    safe_rating = slot_rating + (1.0 - present)[:, None]
    inverse = 1.0 / (safe_rating * safe_rating)
    lodf = tiles.astype(jnp.float32)
    post = slot_flow[:, :, None, :] + lodf[:, None, :, :] * outage_flow[None, :, :, None]
    raised = multipliers + dual_step * (post * post * inverse[:, None, None, :] - 1.0)
    updated = jnp.maximum(raised, 0.0) * present[:, None, None, None]
    weight = updated * post * inverse[:, None, None, :]
    direct = jnp.sum(weight, axis=2)
    line_part = jnp.einsum("bs,shl->hbl", match, direct, precision=lax.Precision.HIGHEST)
    outage_part = jnp.sum(lodf[:, None, :, :] * weight, axis=(0, 3))
    return (updated, line_part, outage_part)


def per_device_general(owned_flow, ratings, lodf_tiles, tile_map, outage_line, block_owner, multipliers):
    hours = owned_flow.shape[1]
    piece = owned_flow.shape[2]
    ctg_count = lax.axis_size("ctg")
    line_count = lax.axis_size("line")
    shard_lines = ratings.shape[0]
    tile = lodf_tiles.shape[-1]
    kblocks = lodf_tiles.shape[0]
    outages = outage_line.shape[0] * ctg_count
    inverse_owner = (
        jnp.zeros_like(block_owner).at[block_owner].set(jnp.arange(ctg_count, dtype=jnp.int32))
    )
    gathered = lax.all_gather(owned_flow, ("ctg", "line"), axis=0, tiled=True)
    shaped = jnp.take(gathered.reshape(ctg_count, line_count, hours, piece), inverse_owner, axis=0)
    every_flow = shaped.transpose(2, 1, 0, 3).reshape(hours, line_count * shard_lines)
    shard_flow = lax.dynamic_slice_in_dim(
        every_flow, lax.axis_index("line") * shard_lines, shard_lines, 1
    )
    outage_flow = jnp.take(every_flow, outage_line, axis=1)
    flow_rows = shard_flow.reshape(hours, shard_lines // tile, tile)
    rating_rows = ratings.reshape(shard_lines // tile, tile)
    outage_blocks = outage_flow.reshape(hours, kblocks, tile).transpose(1, 0, 2)
    updated, line_part, outage_part = jax.vmap(tile_step, in_axes=(0, 0, None, None, 0, 0))(
        lodf_tiles, tile_map, flow_rows, rating_rows, outage_blocks, multipliers
    )
    line_sum = jnp.sum(line_part, axis=0).reshape(hours, shard_lines)
    line_gradient = (
        lax.psum_scatter(
            line_sum.reshape(1, hours, shard_lines), "ctg", scatter_dimension=2, tiled=True
        )
        / outages
    )
    outage_local = outage_part.transpose(1, 0, 2).reshape(hours, kblocks * tile)
    outage_gradient = lax.psum(outage_local, "line") * outage_scale
    return (updated, line_gradient, outage_gradient)


def kernel(
    n_ctg, n_line, outages, hours,
    map_hbm, owner_hbm, outage_hbm, rating_hbm, own_hbm, lodf_hbm, mult_hbm,
    new_ref, line_ref, grad_ref,
    map_ref, owner_ref, ids, rating_ref,
    mult, lodf16, lodf, flows, onehot, slot_flow, slot_half, slot_bar, spread, acc, direct,
    map_send, map_recv, outbox, part, grad,
    small_sem, mult_sem, lodf_sem, own_sem, id_ssem, id_rsem, flow_ssem, flow_rsem, map_ssem, map_rsem,
    part_ssem, part_rsem, dir_ssem, dir_rsem, grad_ssem, grad_rsem,
):
    slots, _, tile, _ = mult.shape
    groups, span = grad.shape[1:3]
    inner = flows.shape[1] // hours
    piece = inner * tile
    me_c = lax.axis_index("ctg")
    me_l = lax.axis_index("line")

    def other_c(d):
        return lax.rem(me_c + d, n_ctg)

    def other_l(d):
        return lax.rem(me_l + d, n_line)

    def to_ctg(src, dst, ssem, rsem, d):
        return pltpu.make_async_remote_copy(
            src_ref=src, dst_ref=dst, send_sem=ssem, recv_sem=rsem,
            device_id={"ctg": other_c(d)}, device_id_type=MESH,
        )

    def to_line(src, dst, ssem, rsem, d):
        return pltpu.make_async_remote_copy(
            src_ref=src, dst_ref=dst, send_sem=ssem, recv_sem=rsem,
            device_id={"line": other_l(d)}, device_id_type=MESH,
        )

    barrier = pltpu.get_barrier_semaphore()
    others = [(dc, dl) for dc in range(n_ctg) for dl in range(n_line) if (dc, dl) != (0, 0)]
    for dc, dl in others:
        pl.semaphore_signal(
            barrier, inc=1, device_id={"ctg": other_c(dc), "line": other_l(dl)}, device_id_type=MESH
        )

    own_copy = pltpu.make_async_copy(own_hbm, flows.at[me_c], own_sem)
    own_copy.start()
    small_copies = [
        pltpu.make_async_copy(src, dst, small_sem.at[i])
        for i, (src, dst) in enumerate(
            ((map_hbm, map_ref), (owner_hbm, owner_ref), (outage_hbm, ids.at[me_c]), (rating_hbm, rating_ref))
        )
    ]
    for copy in small_copies:
        copy.start()
    lodf_copy = pltpu.make_async_copy(lodf_hbm.at[0], lodf16, lodf_sem)
    lodf_copy.start()
    for s in range(slots):
        pltpu.make_async_copy(mult_hbm.at[0, s], mult.at[s], mult_sem.at[s]).start()

    own_copy.wait()
    small_copies[2].wait()
    pl.semaphore_wait(barrier, len(others))

    mine = ids.at[me_c]
    id_copies = [to_ctg(mine, mine, id_ssem.at[d], id_rsem.at[d], d) for d in range(1, n_ctg)]
    for copy in id_copies:
        copy.start()

    far = (2, 1, 3) if n_ctg == 4 else tuple(range(1, n_ctg))
    flow_copies = []
    for g in range(groups):
        rows = flows.at[me_c, pl.ds(g * span * inner, span * inner)]
        copies = [to_ctg(rows, rows, flow_ssem.at[g, d], flow_rsem.at[g, d], d) for d in far]
        for copy in copies:
            copy.start()
        flow_copies.append(copies)
    for i in (0, 1, 3):
        small_copies[i].wait()
    for q in range(n_ctg):
        for i in range(inner):
            map_send[q, pl.ds(i, 1), :] = jnp.full((1, LANES), map_ref[0, q * inner + i], jnp.int32)
    map_copies = []
    for d in range(1, n_ctg):
        copy = to_ctg(map_send.at[other_c(d)], map_recv.at[me_c], map_ssem.at[d], map_rsem.at[d], d)
        copy.start()
        map_copies.append(copy)
    map_recv[me_c] = map_send[me_c]

    for copy in id_copies:
        copy.wait_recv()
    rows_iota = lax.broadcasted_iota(jnp.int32, (tile, LANES), 0)
    base = (me_l * n_ctg + owner_ref[me_c]) * piece
    for c in range(n_ctg):
        wanted = jnp.broadcast_to(ids[c] - base, (tile, LANES))

        def hot_body(b, carry, c=c, wanted=wanted):
            row = pl.multiple_of(b * tile, tile)
            hit = (rows_iota + row) == wanted
            onehot[pl.ds(row, tile), c * tile : (c + 1) * tile] = jnp.where(hit, 1.0, 0.0).astype(jnp.bfloat16)
            return carry

        lax.fori_loop(0, inner, hot_body, 0)
    value = jnp.concatenate(
        [flows[me_c, pl.ds(i, hours, stride=inner), :] for i in range(inner)], axis=1
    )
    value = jnp.concatenate([value, jnp.zeros((16 - hours, piece), jnp.float32)], axis=0)
    high = value.astype(jnp.bfloat16).astype(jnp.float32)
    rest = value - high
    middle = rest.astype(jnp.bfloat16).astype(jnp.float32)
    low = rest - middle
    parts = jnp.concatenate([high, middle, low], axis=0).astype(jnp.bfloat16)
    picked = jnp.dot(parts, onehot[...], preferred_element_type=jnp.float32)
    picked = picked[:16] + picked[16:32] + picked[32:]
    for c in range(n_ctg):
        outbox[c] = picked[:hours, c * tile : (c + 1) * tile]
    part_copies = []
    for dc, dl in others:
        copy = pltpu.make_async_remote_copy(
            src_ref=outbox.at[other_c(dc)], dst_ref=part.at[me_c, me_l],
            send_sem=part_ssem.at[dc, dl], recv_sem=part_rsem.at[dc, dl],
            device_id={"ctg": other_c(dc), "line": other_l(dl)}, device_id_type=MESH,
        )
        copy.start()
        part_copies.append(copy)
    part[me_c, me_l] = outbox[me_c]

    slot_iota = lax.broadcasted_iota(jnp.int32, (slots, LANES), 0)
    rating = jnp.ones((slots, LANES), jnp.float32)
    there = jnp.zeros((slots, LANES), jnp.float32)
    for b in range(n_ctg * inner):
        hit = slot_iota == map_ref[0, b]
        rating = jnp.where(hit, jnp.broadcast_to(rating_ref[pl.ds(b, 1), :], (slots, LANES)), rating)
        there = jnp.where(hit, 1.0, there)
    slot_half[...] = there * (dual_step / (rating * rating))
    slot_bar[...] = jnp.where(there > 0.0, dual_step, 1e30)

    lodf_copy.wait()

    def lodf_body(s, carry):
        lodf[s] = lodf16[s].astype(jnp.float32)
        return carry

    lax.fori_loop(0, slots, lodf_body, 0)
    acc[...] = jnp.zeros_like(acc)

    block_at = []
    for c in range(n_ctg):
        for i in range(inner):
            block = jnp.int32(-1)
            for q in range(n_ctg):
                block = jnp.where(owner_ref[c] == q, map_ref[0, q * inner + i], block)
            block_at.append(block)

    def gather(g):
        for copy in flow_copies[g]:
            copy.wait_recv()
        found = [jnp.zeros((slots, LANES), jnp.float32)] * span
        for c in range(n_ctg):
            for i in range(inner):
                hit = slot_iota == block_at[c * inner + i]
                for t in range(span):
                    row = flows[c, pl.ds((g * span + t) * inner + i, 1), :]
                    found[t] = jnp.where(hit, jnp.broadcast_to(row, (slots, LANES)), found[t])
        for t in range(span):
            slot_flow[g * span + t] = found[t]

    def update(g):
        first = g * span

        def pair_body(p, carry):
            pair = [2 * p, 2 * p + 1]
            if g == 0:
                for s in pair:
                    pltpu.make_async_copy(mult_hbm.at[0, s], mult.at[s], mult_sem.at[s]).wait()

            def lines(ref, s):
                return jnp.broadcast_to(ref[pl.ds(s, 1), :], (ROWS, LANES))

            half = [lines(slot_half, s) for s in pair]
            bar = [lines(slot_bar, s) for s in pair]
            base = [[lines(slot_flow.at[first + t], s) for t in range(span)] for s in pair]

            def row_body(k, sums):
                row = pl.multiple_of(k * ROWS, ROWS)
                rows = pl.ds(row, ROWS)
                factor = [lodf[s, rows, :] for s in pair]
                out = [None] * (2 * span)
                for t in range(span):
                    flow = spread[first + t, rows, :]
                    total = acc[first + t, rows, :]
                    for e, s in enumerate(pair):
                        post = base[e][t] + factor[e] * flow
                        scaled = post * half[e]
                        updated = jnp.maximum(
                            mult[s, first + t, rows, :] + (post * scaled - bar[e]), 0.0
                        )
                        new_ref[s, first + t, rows, :] = updated
                        weight = updated * scaled
                        total = total + factor[e] * weight
                        out[e * span + t] = sums[e * span + t] + weight
                    acc[first + t, rows, :] = total
                return tuple(out)

            zero = jnp.zeros((ROWS, LANES), jnp.float32)
            sums = lax.fori_loop(0, tile // ROWS, row_body, (zero,) * (2 * span), unroll=2)
            for e, s in enumerate(pair):
                for t in range(span):
                    direct[me_c, g, pl.ds(s * span + t, 1), :] = jnp.sum(
                        sums[e * span + t], axis=0, keepdims=True
                    )
            return carry

        lax.fori_loop(0, slots // 2, pair_body, 0)
        mine = direct.at[me_c, g]
        copies = [to_ctg(mine, mine, dir_ssem.at[g, d], dir_rsem.at[g, d], d) for d in far]
        for copy in copies:
            copy.start()
        columns = lax.broadcasted_iota(jnp.int32, (tile, LANES), 1)
        packed = jnp.zeros((tile, LANES), jnp.float32)
        for t in range(span):
            packed = jnp.where(columns == t, jnp.sum(acc[first + t], axis=1, keepdims=True), packed)
        grad[me_l, g] = packed.T[:span]
        return copies

    def combine(g, direct_copies):
        for copy in direct_copies:
            copy.wait_recv()
        for t in range(span):
            total = jnp.zeros((inner, LANES), jnp.float32)
            for c in range(n_ctg):
                which = map_recv[c]
                for s in range(slots):
                    row = direct[c, g, pl.ds(s * span + t, 1), :]
                    total = total + jnp.where(which == s, jnp.broadcast_to(row, (inner, LANES)), 0.0)
            line_ref[pl.ds((g * span + t) * inner, inner), :] = total * (1.0 / dual_step / outages)

    for copy in part_copies:
        copy.wait_recv()
    outage = jnp.zeros((hours, LANES), jnp.float32)
    for c in range(n_ctg):
        for j in range(n_line):
            outage = outage + part[c, j]
    turned = jnp.concatenate([outage, jnp.zeros((16 - hours, LANES), jnp.float32)], axis=0).T
    for t in range(hours):
        spread[t] = jnp.broadcast_to(turned[:, t : t + 1], (tile, LANES))

    direct_copies = []
    for g in range(groups):
        gather(g)
        direct_copies.append(update(g))

    mine = grad.at[me_l]
    grad_copies = [to_line(mine, mine, grad_ssem.at[d], grad_rsem.at[d], d) for d in range(1, n_line)]
    for copy in grad_copies:
        copy.start()

    for copy in map_copies:
        copy.wait_recv()
    for g in range(groups):
        combine(g, direct_copies[g])

    for copy in grad_copies:
        copy.wait_recv()
    for g in range(groups):
        total = grad[0, g]
        for j in range(1, n_line):
            total = total + grad[j, g]
        grad_ref[pl.ds(g * span, span), :] = total * (outage_scale / dual_step)

    for copies in flow_copies + direct_copies + [id_copies, map_copies, part_copies, grad_copies]:
        for copy in copies:
            copy.wait_send()


def write_out(new_vmem, line_vmem, grad_vmem, new_hbm, line_hbm, grad_hbm, sems):
    slots = new_vmem.shape[0]
    copies = [pltpu.make_async_copy(new_vmem.at[s], new_hbm.at[s], sems.at[s]) for s in range(slots)]
    copies.append(pltpu.make_async_copy(line_vmem, line_hbm, sems.at[slots]))
    copies.append(pltpu.make_async_copy(grad_vmem, grad_hbm, sems.at[slots + 1]))
    for copy in copies:
        copy.start()
    for copy in copies:
        copy.wait()


def per_device_fused(owned_flow, ratings, lodf_tiles, tile_map, outage_line, block_owner, multipliers):
    n_ctg = lax.axis_size("ctg")
    n_line = lax.axis_size("line")
    _, hours, piece = owned_flow.shape
    _, slots, tile, _ = lodf_tiles.shape
    inner = piece // tile
    outages = outage_line.shape[0] * n_ctg
    span = 4
    groups = hours // span
    f32, bf16, i32 = jnp.float32, jnp.bfloat16, jnp.int32
    dma = pltpu.SemaphoreType.DMA
    vmem = pl.BlockSpec(memory_space=pltpu.VMEM)
    hbm = pl.BlockSpec(memory_space=pltpu.HBM)
    shapes = (
        jax.ShapeDtypeStruct((slots, hours, tile, tile), f32),
        jax.ShapeDtypeStruct((hours * inner, tile), f32),
        jax.ShapeDtypeStruct((hours, tile), f32),
    )
    results = pl.pallas_call(
        functools.partial(kernel, n_ctg, n_line, outages, hours),
        out_shape=shapes,
        in_specs=[hbm] * 7,
        out_specs=(vmem, vmem, vmem),
        scratch_shapes=[
            pltpu.SMEM(tile_map.shape, i32),
            pltpu.SMEM(block_owner.shape, i32),
            pltpu.VMEM((n_ctg, 1, tile), i32),
            pltpu.VMEM((n_ctg * inner, tile), f32),
            pltpu.VMEM((slots, hours, tile, tile), f32),
            pltpu.VMEM((slots, tile, tile), bf16),
            pltpu.VMEM((slots, tile, tile), f32),
            pltpu.VMEM((n_ctg, hours * inner, tile), f32),
            pltpu.VMEM((piece, n_ctg * tile), bf16),
            pltpu.VMEM((hours, slots, tile), f32),
            pltpu.VMEM((slots, tile), f32),
            pltpu.VMEM((slots, tile), f32),
            pltpu.VMEM((hours, tile, tile), f32),
            pltpu.VMEM((hours, tile, tile), f32),
            pltpu.VMEM((n_ctg, groups, slots * span, tile), f32),
            pltpu.VMEM((n_ctg, inner, tile), i32),
            pltpu.VMEM((n_ctg, inner, tile), i32),
            pltpu.VMEM((n_ctg, hours, tile), f32),
            pltpu.VMEM((n_ctg, n_line, hours, tile), f32),
            pltpu.VMEM((n_line, groups, span, tile), f32),
            dma((4,)), dma((slots,)), dma, dma,
            dma((n_ctg,)), dma((n_ctg,)),
            dma((groups, n_ctg)), dma((groups, n_ctg)), dma((n_ctg,)), dma((n_ctg,)),
            dma((n_ctg, n_line)), dma((n_ctg, n_line)),
            dma((groups, n_ctg)), dma((groups, n_ctg)),
            dma((n_line,)), dma((n_line,)),
        ],
        compiler_params=pltpu.CompilerParams(
            collective_id=0, has_side_effects=True, vmem_limit_bytes=40 * 1024 * 1024
        ),
        name="dual_step",
    )(
        *(
            pltpu.with_memory_space_constraint(x, pltpu.HBM)
            for x in (
                tile_map, block_owner, outage_line.reshape(1, tile),
                ratings.reshape(n_ctg * inner, tile), owned_flow.reshape(hours * inner, tile),
                lodf_tiles, multipliers,
            )
        )
    )
    updated, line_gradient, outage_gradient = pl.pallas_call(
        write_out,
        out_shape=shapes,
        in_specs=[vmem] * 3,
        out_specs=(hbm,) * 3,
        scratch_shapes=[dma((slots + 2,))],
        compiler_params=pltpu.CompilerParams(vmem_limit_bytes=40 * 1024 * 1024),
        name="write_out",
    )(*(pltpu.with_memory_space_constraint(x, pltpu.VMEM) for x in results))
    return updated[None], line_gradient.reshape(1, hours, piece), outage_gradient


def per_device(owned_flow, ratings, lodf_tiles, tile_map, outage_line, block_owner, multipliers):
    n_ctg = lax.axis_size("ctg")
    tile = lodf_tiles.shape[-1]
    whole = (
        tile == LANES
        and owned_flow.shape[1] % 4 == 0
        and owned_flow.shape[1] <= 12
        and lodf_tiles.shape[1] == 8
        and owned_flow.shape[2] % tile == 0
        and outage_line.shape[0] == tile
        and lodf_tiles.shape[0] == 1
        and n_ctg <= 4
    )
    form = per_device_fused if whole else per_device_general
    return form(owned_flow, ratings, lodf_tiles, tile_map, outage_line, block_owner, multipliers)


def solution(mesh):
    placed = (
        P("line", "grp", "ctg"),
        P("line"),
        P("ctg", "line", None, None),
        P("ctg", "line"),
        P("ctg"),
        P(),
        P("ctg", "line", "grp", None, None),
    )
    return jax.shard_map(
        per_device,
        mesh=mesh,
        in_specs=placed,
        out_specs=(P("ctg", "line", "grp", None, None), P("line", "grp", "ctg"), P("grp", "ctg")),
        check_vma=False,
    )
```

```python
import functools

import jax
import jax.numpy as jnp
from jax import lax
from jax.experimental import pallas as pl
from jax.experimental.pallas import tpu as pltpu
from jax.sharding import PartitionSpec as P

dual_step = 0.5
outage_scale = 0.0625
MESH = pl.DeviceIdType.MESH
LANES = 128
ROWS = 8


def tile_step(tiles, slot_map, flow_rows, rating_rows, outage_flow, multipliers):
    slots = tiles.shape[0]
    match = (slot_map[:, None] == jnp.arange(slots, dtype=jnp.int32)[None, :]).astype(jnp.float32)
    slot_flow = jnp.einsum("bs,hbl->shl", match, flow_rows, precision=lax.Precision.HIGHEST)
    slot_rating = jnp.einsum("bs,bl->sl", match, rating_rows, precision=lax.Precision.HIGHEST)
    present = jnp.sum(match, axis=0)
    safe_rating = slot_rating + (1.0 - present)[:, None]
    inverse = 1.0 / (safe_rating * safe_rating)
    lodf = tiles.astype(jnp.float32)
    post = slot_flow[:, :, None, :] + lodf[:, None, :, :] * outage_flow[None, :, :, None]
    raised = multipliers + dual_step * (post * post * inverse[:, None, None, :] - 1.0)
    updated = jnp.maximum(raised, 0.0) * present[:, None, None, None]
    weight = updated * post * inverse[:, None, None, :]
    direct = jnp.sum(weight, axis=2)
    line_part = jnp.einsum("bs,shl->hbl", match, direct, precision=lax.Precision.HIGHEST)
    outage_part = jnp.sum(lodf[:, None, :, :] * weight, axis=(0, 3))
    return (updated, line_part, outage_part)


def per_device_general(owned_flow, ratings, lodf_tiles, tile_map, outage_line, block_owner, multipliers):
    hours = owned_flow.shape[1]
    piece = owned_flow.shape[2]
    ctg_count = lax.axis_size("ctg")
    line_count = lax.axis_size("line")
    shard_lines = ratings.shape[0]
    tile = lodf_tiles.shape[-1]
    kblocks = lodf_tiles.shape[0]
    outages = outage_line.shape[0] * ctg_count
    inverse_owner = (
        jnp.zeros_like(block_owner).at[block_owner].set(jnp.arange(ctg_count, dtype=jnp.int32))
    )
    gathered = lax.all_gather(owned_flow, ("ctg", "line"), axis=0, tiled=True)
    shaped = jnp.take(gathered.reshape(ctg_count, line_count, hours, piece), inverse_owner, axis=0)
    every_flow = shaped.transpose(2, 1, 0, 3).reshape(hours, line_count * shard_lines)
    shard_flow = lax.dynamic_slice_in_dim(
        every_flow, lax.axis_index("line") * shard_lines, shard_lines, 1
    )
    outage_flow = jnp.take(every_flow, outage_line, axis=1)
    flow_rows = shard_flow.reshape(hours, shard_lines // tile, tile)
    rating_rows = ratings.reshape(shard_lines // tile, tile)
    outage_blocks = outage_flow.reshape(hours, kblocks, tile).transpose(1, 0, 2)
    updated, line_part, outage_part = jax.vmap(tile_step, in_axes=(0, 0, None, None, 0, 0))(
        lodf_tiles, tile_map, flow_rows, rating_rows, outage_blocks, multipliers
    )
    line_sum = jnp.sum(line_part, axis=0).reshape(hours, shard_lines)
    line_gradient = (
        lax.psum_scatter(
            line_sum.reshape(1, hours, shard_lines), "ctg", scatter_dimension=2, tiled=True
        )
        / outages
    )
    outage_local = outage_part.transpose(1, 0, 2).reshape(hours, kblocks * tile)
    outage_gradient = lax.psum(outage_local, "line") * outage_scale
    return (updated, line_gradient, outage_gradient)


def kernel(
    n_ctg, n_line, outages, hours,
    map_hbm, owner_hbm, outage_hbm, rating_hbm, own_hbm, lodf_hbm, mult_hbm,
    new_ref, line_ref, grad_ref,
    map_ref, owner_ref, outage_ref, rating_ref,
    mult, lodf16, lodf, flows, onehot, slot_flow, slot_half, slot_bar, spread, acc, direct,
    map_send, map_recv, part, grad,
    small_sem, mult_sem, lodf_sem, own_sem, flow_ssem, flow_rsem, map_ssem, map_rsem,
    part_ssem, part_rsem, dir_ssem, dir_rsem, grad_ssem, grad_rsem,
):
    slots, _, tile, _ = mult.shape
    groups, span = part.shape[1:3]
    inner = flows.shape[1] // hours
    piece = inner * tile
    me_c = lax.axis_index("ctg")
    me_l = lax.axis_index("line")

    def other_c(d):
        return lax.rem(me_c + d, n_ctg)

    def other_l(d):
        return lax.rem(me_l + d, n_line)

    def to_ctg(src, dst, ssem, rsem, d):
        return pltpu.make_async_remote_copy(
            src_ref=src, dst_ref=dst, send_sem=ssem, recv_sem=rsem,
            device_id={"ctg": other_c(d)}, device_id_type=MESH,
        )

    def to_line(src, dst, ssem, rsem, d):
        return pltpu.make_async_remote_copy(
            src_ref=src, dst_ref=dst, send_sem=ssem, recv_sem=rsem,
            device_id={"line": other_l(d)}, device_id_type=MESH,
        )

    barrier = pltpu.get_barrier_semaphore()
    for d in range(1, n_ctg):
        pl.semaphore_signal(barrier, inc=1, device_id={"ctg": other_c(d)}, device_id_type=MESH)
    for d in range(1, n_line):
        pl.semaphore_signal(barrier, inc=1, device_id={"line": other_l(d)}, device_id_type=MESH)

    own_copy = pltpu.make_async_copy(own_hbm, flows.at[me_c], own_sem)
    own_copy.start()
    small_copies = [
        pltpu.make_async_copy(src, dst, small_sem.at[i])
        for i, (src, dst) in enumerate(
            ((map_hbm, map_ref), (owner_hbm, owner_ref), (outage_hbm, outage_ref), (rating_hbm, rating_ref))
        )
    ]
    for copy in small_copies:
        copy.start()
    lodf_copy = pltpu.make_async_copy(lodf_hbm.at[0], lodf16, lodf_sem)
    lodf_copy.start()
    for s in range(slots):
        pltpu.make_async_copy(mult_hbm.at[0, s], mult.at[s], mult_sem.at[s]).start()

    own_copy.wait()
    pl.semaphore_wait(barrier, n_ctg - 1 + n_line - 1)

    far = (2, 1, 3) if n_ctg == 4 else tuple(range(1, n_ctg))
    flow_copies = []
    for g in range(groups):
        rows = flows.at[me_c, pl.ds(g * span * inner, span * inner)]
        copies = [to_ctg(rows, rows, flow_ssem.at[g, d], flow_rsem.at[g, d], d) for d in far]
        for copy in copies:
            copy.start()
        flow_copies.append(copies)
    for copy in small_copies:
        copy.wait()
    for q in range(n_ctg):
        for i in range(inner):
            map_send[q, pl.ds(i, 1), :] = jnp.full((1, LANES), map_ref[0, q * inner + i], jnp.int32)
    map_copies = []
    for d in range(1, n_ctg):
        copy = to_ctg(map_send.at[other_c(d)], map_recv.at[me_c], map_ssem.at[d], map_rsem.at[d], d)
        copy.start()
        map_copies.append(copy)
    map_recv[me_c] = map_send[me_c]

    rows_iota = lax.broadcasted_iota(jnp.int32, (tile, LANES), 0)
    for c in range(n_ctg):
        base = (me_l * n_ctg + owner_ref[c]) * piece
        wanted = jnp.broadcast_to(outage_ref[...] - base, (tile, LANES))

        def hot_body(b, carry, c=c, wanted=wanted):
            row = pl.multiple_of(b * tile, tile)
            hit = (rows_iota + row) == wanted
            onehot[c, pl.ds(row, tile), :] = jnp.where(hit, 1.0, 0.0).astype(jnp.bfloat16)
            return carry

        lax.fori_loop(0, inner, hot_body, 0)

    slot_iota = lax.broadcasted_iota(jnp.int32, (slots, LANES), 0)
    rating = jnp.ones((slots, LANES), jnp.float32)
    there = jnp.zeros((slots, LANES), jnp.float32)
    for b in range(n_ctg * inner):
        hit = slot_iota == map_ref[0, b]
        rating = jnp.where(hit, jnp.broadcast_to(rating_ref[pl.ds(b, 1), :], (slots, LANES)), rating)
        there = jnp.where(hit, 1.0, there)
    slot_half[...] = there * (dual_step / (rating * rating))
    slot_bar[...] = jnp.where(there > 0.0, dual_step, 1e30)

    lodf_copy.wait()

    def lodf_body(s, carry):
        lodf[s] = lodf16[s].astype(jnp.float32)
        return carry

    lax.fori_loop(0, slots, lodf_body, 0)
    acc[...] = jnp.zeros_like(acc)

    block_at = []
    for c in range(n_ctg):
        for i in range(inner):
            block = jnp.int32(-1)
            for q in range(n_ctg):
                block = jnp.where(owner_ref[c] == q, map_ref[0, q * inner + i], block)
            block_at.append(block)

    def pick(c, g):
        value = jnp.concatenate(
            [flows[c, pl.ds(g * span * inner + i, span, stride=inner), :] for i in range(inner)], axis=1
        )
        high = value.astype(jnp.bfloat16).astype(jnp.float32)
        rest = value - high
        middle = rest.astype(jnp.bfloat16).astype(jnp.float32)
        low = rest - middle
        parts = jnp.concatenate([high, middle, low, jnp.zeros_like(low)], axis=0).astype(jnp.bfloat16)
        total = jnp.dot(parts, onehot[c], preferred_element_type=jnp.float32)
        return total[:span] + total[span : 2 * span] + total[2 * span : 3 * span]

    def gather(g):
        for copy in flow_copies[g]:
            copy.wait_recv()
        picked = pick(0, g)
        for c in range(1, n_ctg):
            picked = picked + pick(c, g)
        part[me_l, g] = picked
        mine = part.at[me_l, g]
        copies = [
            to_line(mine, mine, part_ssem.at[g, d], part_rsem.at[g, d], d) for d in range(1, n_line)
        ]
        for copy in copies:
            copy.start()
        found = [jnp.zeros((slots, LANES), jnp.float32)] * span
        for c in range(n_ctg):
            for i in range(inner):
                hit = slot_iota == block_at[c * inner + i]
                for t in range(span):
                    row = flows[c, pl.ds((g * span + t) * inner + i, 1), :]
                    found[t] = jnp.where(hit, jnp.broadcast_to(row, (slots, LANES)), found[t])
        for t in range(span):
            slot_flow[g * span + t] = found[t]
        return copies

    def update(g, part_copies):
        for copy in part_copies:
            copy.wait_recv()
        outage = part[0, g]
        for j in range(1, n_line):
            outage = outage + part[j, g]
        turned = jnp.concatenate([outage, jnp.zeros((ROWS - span, LANES), jnp.float32)], axis=0).T
        for t in range(span):
            spread[t] = jnp.broadcast_to(turned[:, t : t + 1], (tile, LANES))
        first = g * span

        def pair_body(p, carry):
            pair = [2 * p, 2 * p + 1]
            if g == 0:
                for s in pair:
                    pltpu.make_async_copy(mult_hbm.at[0, s], mult.at[s], mult_sem.at[s]).wait()

            def lines(ref, s):
                return jnp.broadcast_to(ref[pl.ds(s, 1), :], (ROWS, LANES))

            half = [lines(slot_half, s) for s in pair]
            bar = [lines(slot_bar, s) for s in pair]
            base = [[lines(slot_flow.at[first + t], s) for t in range(span)] for s in pair]

            def row_body(k, sums):
                row = pl.multiple_of(k * ROWS, ROWS)
                rows = pl.ds(row, ROWS)
                factor = [lodf[s, rows, :] for s in pair]
                out = [None] * (2 * span)
                for t in range(span):
                    flow = spread[t, rows, :]
                    total = acc[first + t, rows, :]
                    for e, s in enumerate(pair):
                        post = base[e][t] + factor[e] * flow
                        scaled = post * half[e]
                        updated = jnp.maximum(
                            mult[s, first + t, rows, :] + (post * scaled - bar[e]), 0.0
                        )
                        new_ref[s, first + t, rows, :] = updated
                        weight = updated * scaled
                        total = total + factor[e] * weight
                        out[e * span + t] = sums[e * span + t] + weight
                    acc[first + t, rows, :] = total
                return tuple(out)

            zero = jnp.zeros((ROWS, LANES), jnp.float32)
            sums = lax.fori_loop(0, tile // ROWS, row_body, (zero,) * (2 * span), unroll=2)
            for e, s in enumerate(pair):
                for t in range(span):
                    direct[me_c, g, pl.ds(s * span + t, 1), :] = jnp.sum(
                        sums[e * span + t], axis=0, keepdims=True
                    )
            return carry

        lax.fori_loop(0, slots // 2, pair_body, 0)
        mine = direct.at[me_c, g]
        copies = [to_ctg(mine, mine, dir_ssem.at[g, d], dir_rsem.at[g, d], d) for d in far]
        for copy in copies:
            copy.start()
        columns = lax.broadcasted_iota(jnp.int32, (tile, LANES), 1)
        packed = jnp.zeros((tile, LANES), jnp.float32)
        for t in range(span):
            packed = jnp.where(columns == t, jnp.sum(acc[first + t], axis=1, keepdims=True), packed)
        grad[me_l, g] = packed.T[:span]
        return copies

    def combine(g, direct_copies):
        for copy in direct_copies:
            copy.wait_recv()
        for t in range(span):
            total = jnp.zeros((inner, LANES), jnp.float32)
            for c in range(n_ctg):
                which = map_recv[c]
                for s in range(slots):
                    row = direct[c, g, pl.ds(s * span + t, 1), :]
                    total = total + jnp.where(which == s, jnp.broadcast_to(row, (inner, LANES)), 0.0)
            line_ref[pl.ds((g * span + t) * inner, inner), :] = total * (1.0 / dual_step / outages)

    part_copies, direct_copies = [], []
    for g in range(groups):
        part_copies.append(gather(g))
        if g >= 1:
            direct_copies.append(update(g - 1, part_copies[g - 1]))
    direct_copies.append(update(groups - 1, part_copies[groups - 1]))

    mine = grad.at[me_l]
    grad_copies = [to_line(mine, mine, grad_ssem.at[d], grad_rsem.at[d], d) for d in range(1, n_line)]
    for copy in grad_copies:
        copy.start()

    for copy in map_copies:
        copy.wait_recv()
    for g in range(groups):
        combine(g, direct_copies[g])

    for copy in grad_copies:
        copy.wait_recv()
    for g in range(groups):
        total = grad[0, g]
        for j in range(1, n_line):
            total = total + grad[j, g]
        grad_ref[pl.ds(g * span, span), :] = total * (outage_scale / dual_step)

    for copies in flow_copies + part_copies + direct_copies + [map_copies, grad_copies]:
        for copy in copies:
            copy.wait_send()


def write_out(new_vmem, line_vmem, grad_vmem, new_hbm, line_hbm, grad_hbm, sems):
    slots = new_vmem.shape[0]
    copies = [pltpu.make_async_copy(new_vmem.at[s], new_hbm.at[s], sems.at[s]) for s in range(slots)]
    copies.append(pltpu.make_async_copy(line_vmem, line_hbm, sems.at[slots]))
    copies.append(pltpu.make_async_copy(grad_vmem, grad_hbm, sems.at[slots + 1]))
    for copy in copies:
        copy.start()
    for copy in copies:
        copy.wait()


def per_device_fused(owned_flow, ratings, lodf_tiles, tile_map, outage_line, block_owner, multipliers):
    n_ctg = lax.axis_size("ctg")
    n_line = lax.axis_size("line")
    _, hours, piece = owned_flow.shape
    _, slots, tile, _ = lodf_tiles.shape
    inner = piece // tile
    outages = outage_line.shape[0] * n_ctg
    span = 4
    groups = hours // span
    f32, bf16, i32 = jnp.float32, jnp.bfloat16, jnp.int32
    dma = pltpu.SemaphoreType.DMA
    vmem = pl.BlockSpec(memory_space=pltpu.VMEM)
    hbm = pl.BlockSpec(memory_space=pltpu.HBM)
    shapes = (
        jax.ShapeDtypeStruct((slots, hours, tile, tile), f32),
        jax.ShapeDtypeStruct((hours * inner, tile), f32),
        jax.ShapeDtypeStruct((hours, tile), f32),
    )
    results = pl.pallas_call(
        functools.partial(kernel, n_ctg, n_line, outages, hours),
        out_shape=shapes,
        in_specs=[hbm] * 7,
        out_specs=(vmem, vmem, vmem),
        scratch_shapes=[
            pltpu.SMEM(tile_map.shape, i32),
            pltpu.SMEM(block_owner.shape, i32),
            pltpu.VMEM((1, tile), i32),
            pltpu.VMEM((n_ctg * inner, tile), f32),
            pltpu.VMEM((slots, hours, tile, tile), f32),
            pltpu.VMEM((slots, tile, tile), bf16),
            pltpu.VMEM((slots, tile, tile), f32),
            pltpu.VMEM((n_ctg, hours * inner, tile), f32),
            pltpu.VMEM((n_ctg, piece, tile), bf16),
            pltpu.VMEM((hours, slots, tile), f32),
            pltpu.VMEM((slots, tile), f32),
            pltpu.VMEM((slots, tile), f32),
            pltpu.VMEM((span, tile, tile), f32),
            pltpu.VMEM((hours, tile, tile), f32),
            pltpu.VMEM((n_ctg, groups, slots * span, tile), f32),
            pltpu.VMEM((n_ctg, inner, tile), i32),
            pltpu.VMEM((n_ctg, inner, tile), i32),
            pltpu.VMEM((n_line, groups, span, tile), f32),
            pltpu.VMEM((n_line, groups, span, tile), f32),
            dma((4,)), dma((slots,)), dma, dma,
            dma((groups, n_ctg)), dma((groups, n_ctg)), dma((n_ctg,)), dma((n_ctg,)),
            dma((groups, n_line)), dma((groups, n_line)),
            dma((groups, n_ctg)), dma((groups, n_ctg)),
            dma((n_line,)), dma((n_line,)),
        ],
        compiler_params=pltpu.CompilerParams(
            collective_id=0, has_side_effects=True, vmem_limit_bytes=40 * 1024 * 1024
        ),
        name="dual_step",
    )(
        *(
            pltpu.with_memory_space_constraint(x, pltpu.HBM)
            for x in (
                tile_map, block_owner, outage_line.reshape(1, tile),
                ratings.reshape(n_ctg * inner, tile), owned_flow.reshape(hours * inner, tile),
                lodf_tiles, multipliers,
            )
        )
    )
    updated, line_gradient, outage_gradient = pl.pallas_call(
        write_out,
        out_shape=shapes,
        in_specs=[vmem] * 3,
        out_specs=(hbm,) * 3,
        scratch_shapes=[dma((slots + 2,))],
        compiler_params=pltpu.CompilerParams(vmem_limit_bytes=40 * 1024 * 1024),
        name="write_out",
    )(*(pltpu.with_memory_space_constraint(x, pltpu.VMEM) for x in results))
    return updated[None], line_gradient.reshape(1, hours, piece), outage_gradient


def per_device(owned_flow, ratings, lodf_tiles, tile_map, outage_line, block_owner, multipliers):
    n_ctg = lax.axis_size("ctg")
    tile = lodf_tiles.shape[-1]
    whole = (
        tile == LANES
        and owned_flow.shape[1] % 4 == 0
        and lodf_tiles.shape[1] == 8
        and owned_flow.shape[2] % tile == 0
        and outage_line.shape[0] == tile
        and lodf_tiles.shape[0] == 1
        and n_ctg <= 4
    )
    form = per_device_fused if whole else per_device_general
    return form(owned_flow, ratings, lodf_tiles, tile_map, outage_line, block_owner, multipliers)


def solution(mesh):
    placed = (
        P("line", "grp", "ctg"),
        P("line"),
        P("ctg", "line", None, None),
        P("ctg", "line"),
        P("ctg"),
        P(),
        P("ctg", "line", "grp", None, None),
    )
    return jax.shard_map(
        per_device,
        mesh=mesh,
        in_specs=placed,
        out_specs=(P("ctg", "line", "grp", None, None), P("line", "grp", "ctg"), P("grp", "ctg")),
        check_vma=False,
    )
```
